512 devices in a mesh: row: 16 (over z), col: 8 (over y, x_lo), rep: 4 (over x_hi, core).
Axes of the slice: x: 4 (x_hi: 2, x_lo: 2; x = x_hi * 2 + x_lo), y: 4, z: 16, core: 2. Of those that a mesh axis runs over, the one named last changes fastest.
Arguments:
- tokens: bfloat16 [4, 256, 16384], P('rep', 'col', 'row'), may hold values from -6 to 6
- out_grad: bfloat16 [4, 256, 8192], P('rep', 'row', 'col'), may hold values from -0.1875 to 0.1875
- moment_old: float32 [16384, 8192], P(('row', 'rep'), 'col'), may hold values from -6 to 6
- basis_old: float32 [16384, 512], P(('row', 'rep')), may hold values from -16 to 16
- factor_old: float32 [8192, 512], P('col', 'row'), may hold values from -12 to 12
- test_matrix: bfloat16 [8192, 512], P('col'), may hold values from -6 to 6
Outputs:
- moment: float32 [16384, 8192], P(('row', 'rep'), 'col')
- basis_new: float32 [16384, 512], P(('row', 'rep'))
- factor_new: float32 [8192, 512], P('col', 'row')
The draws below stay inside these ranges and needn't reach their ends.
All inputs are finite; a program needn't handle non-finite values.
Results may differ from the reference program's by a relative error of at most 0.017.
Values may be sent and summed in bfloat16 or wider, within the bound.
A program may use at most 64 MiB of HBM per device.

```python
import jax
import jax.numpy as jnp
from jax import lax

R = 16384
C = 8192
K = 512
TOK_BLOCK = 256
TOKENS = 1024
N_REP = 4


def row_profile():
    position = (jnp.arange(R, dtype=jnp.float32) + 1.0) / R
    return 0.5 + 6.0 * position ** 12


def draw_basis_old(key, part):
    key = jax.random.fold_in(key, 11)
    values = jax.random.truncated_normal(key, -4.0, 4.0, (R, K), jnp.float32)
    return values * row_profile()[:, None] / jnp.sqrt(jnp.float32(R))


def steps_of(key, extent, pieces, least, high):
    factor_of = 1.0
    for dim, blocks in pieces:
        heights = jax.random.uniform(jax.random.fold_in(jax.random.fold_in(key, 6), dim), (blocks,), jnp.float32, least / len(pieces), high / len(pieces))
        factor_of = factor_of * jnp.repeat(jnp.exp(heights), extent[dim] // blocks).reshape((-1,) + (1,) * (len(extent) - 1 - dim))
    return factor_of


def scatter_about(own_key, shape, scale, bound, split=(), held_as=jnp.bfloat16):
    values = jax.random.normal(own_key, shape, jnp.float32) * scale
    if len(split) > 0:
        values = steps_of(own_key, shape, split, -0.22, 0.18) * values
    return jnp.clip(values, min=-bound, max=bound).astype(held_as)


def setup_inputs(seed: int = 0) -> dict:
    arg_keys = jax.random.split(jax.random.key(seed), 7)
    tokens = scatter_about(arg_keys[0], (N_REP, TOK_BLOCK, R), 1.0, 6.0, ((0, 4), (1, 8), (2, 16)))
    out_grad = scatter_about(arg_keys[1], (N_REP, TOK_BLOCK, C), TOKENS ** -0.5, 0.1875, ((0, 4), (1, 16), (2, 8)))
    moment_old = scatter_about(arg_keys[2], (R, C), 1.0, 6.0, ((0, 64), (1, 8)), jnp.float32)
    basis_old = draw_basis_old(jax.random.fold_in(arg_keys[6], 71), 0)
    factor_old = scatter_about(arg_keys[4], (C, K), 2.0, 12.0, ((0, 8), (1, 16)), jnp.float32)
    test_matrix = scatter_about(arg_keys[5], (C, K), 1.0, 6.0, ((0, 8),))
    return {"tokens": tokens, "out_grad": out_grad, "moment_old": moment_old, "basis_old": basis_old, "factor_old": factor_old, "test_matrix": test_matrix}


def reference(tokens, out_grad, moment_old, basis_old, factor_old, test_matrix):
    gradient = jnp.zeros((R, C), jnp.float32)
    for block in range(N_REP):
        partial_value = lax.dot_general(tokens[block].astype(jnp.float32), out_grad[block].astype(jnp.float32), (((0,), (0,)), ((), ())), preferred_element_type=jnp.float32)
        partial_value = lax.optimization_barrier(partial_value.astype(jnp.bfloat16))
        gradient = gradient + partial_value.astype(jnp.float32)
    moment = 0.9 * moment_old + 0.1 * gradient
    previous = jnp.dot(basis_old, factor_old.T, precision=lax.Precision.HIGHEST)
    second = (0.95 * previous + 0.05 * gradient * gradient).astype(jnp.bfloat16)
    sketch = jnp.dot(second.astype(jnp.float32), test_matrix.astype(jnp.float32), preferred_element_type=jnp.float32)
    gram_matrix = jnp.dot(sketch.T, sketch, precision=lax.Precision.HIGHEST)
    ridge_shift = 0.01 * jnp.trace(gram_matrix) / K
    lower_factor = jnp.linalg.cholesky(gram_matrix + ridge_shift * jnp.eye(K, dtype=jnp.float32))
    orthonormal = jax.scipy.linalg.solve_triangular(lower_factor, sketch.T, lower=True).T
    basis_new = orthonormal
    basis_bf = orthonormal.astype(jnp.bfloat16)
    factor_new = lax.dot_general(second.astype(jnp.float32), basis_bf.astype(jnp.float32), (((0,), (0,)), ((), ())), preferred_element_type=jnp.float32)
    return (moment, basis_new, factor_new)
```

```python
import functools

import jax
import jax.numpy as jnp
from jax import lax
from jax.experimental import pallas as pl
from jax.experimental.pallas import tpu as pltpu
from jax.sharding import PartitionSpec as P

MESH = pl.DeviceIdType.MESH
F32 = jnp.float32
BF16 = jnp.bfloat16
N_ROW, N_COL, N_REP = 16, 8, 4


def remote(src, dst, send, recv, device):
    return pltpu.make_async_remote_copy(
        src_ref=src, dst_ref=dst, send_sem=send, recv_sem=recv, device_id=device, device_id_type=MESH
    )


def greet(devices):
    barrier = pltpu.get_barrier_semaphore()
    for device in devices:
        pl.semaphore_signal(barrier, inc=1, device_id=device, device_id_type=MESH)
    pl.semaphore_wait(barrier, len(devices))


def others(axis, size):
    me = lax.axis_index(axis)
    return [{axis: lax.rem(me + o, size)} for o in range(1, size)]


def sketch_kernel(x_ref, out_ref, landed, send1, recv1, send2, recv2):
    me = lax.axis_index("col")
    peers = others("col", N_COL)
    greet(peers)
    rows = x_ref.shape[0] // N_COL
    first = []
    for o, peer in enumerate(peers):
        start = pl.multiple_of(peer["col"] * rows, rows)
        copy = remote(x_ref.at[pl.ds(start, rows)], landed.at[o], send1.at[o], recv1.at[o], peer)
        copy.start()
        first.append(copy)
    mine = pl.ds(pl.multiple_of(me * rows, rows), rows)
    total = x_ref[mine]
    for o in range(N_COL - 1):
        first[o].wait_recv()
        total = total + landed[o]
    out_ref[mine] = total
    second = []
    for o, peer in enumerate(peers):
        copy = remote(out_ref.at[mine], out_ref.at[mine], send2.at[o], recv2.at[o], peer)
        copy.start()
        second.append(copy)
    for copy in first:
        copy.wait_send()
    for copy in second:
        copy.wait()


def sum_sketch(x):
    rows = x.shape[0] // N_COL
    n = N_COL - 1
    return pl.pallas_call(
        sketch_kernel,
        out_shape=jax.ShapeDtypeStruct(x.shape, F32),
        in_specs=[pl.BlockSpec(memory_space=pltpu.VMEM)],
        out_specs=pl.BlockSpec(memory_space=pltpu.VMEM),
        scratch_shapes=[pltpu.VMEM((n, rows, x.shape[1]), F32)] + [pltpu.SemaphoreType.DMA((n,))] * 4,
        compiler_params=pltpu.CompilerParams(collective_id=1, has_side_effects=True, vmem_limit_bytes=32 << 20),
        name="sum_sketch",
    )(x)


def gram_kernel(x_ref, out_ref, land1, tiles, land2, s1, r1, s2, r2, s3, r3, s4, r4, s5, r5):
    row, col, rep = lax.axis_index("row"), lax.axis_index("col"), lax.axis_index("rep")
    half, core = rep // 2, lax.rem(rep, 2)
    rep_peers = others("rep", N_REP)
    row_peers = others("row", N_ROW)
    plane = []
    for h in range(2):
        for o in range(N_COL):
            if h or o:
                plane.append({"col": lax.rem(col + o, N_COL), "rep": lax.rem(half + h, 2) * 2 + core})
    sibling = {"rep": half * 2 + 1 - core}
    greet(rep_peers + row_peers + plane)

    copies = []
    for o, peer in enumerate(rep_peers):
        start = pl.multiple_of(peer["rep"] * 16, 16)
        copy = remote(x_ref.at[pl.ds(start, 16)], land1.at[o], s1.at[o], r1.at[o], peer)
        copy.start()
        copies.append(copy)
    total = x_ref[pl.ds(pl.multiple_of(rep * 16, 16), 16)]
    for o in range(N_REP - 1):
        copies[o].wait_recv()
        total = total + land1[o]
    for t in range(8):
        tiles[t] = total[8 * (t // 4) : 8 * (t // 4) + 8, 128 * (t % 4) : 128 * (t % 4) + 128]

    mine = lax.rem(row, 8)
    for o, peer in enumerate(row_peers):
        copy = remote(tiles.at[lax.rem(peer["row"], 8)], land2.at[row], s2.at[o], r2.at[o], peer)
        copy.start()
        copies.append(copy)
    land2[row] = tiles[mine]
    for o in range(N_ROW - 1):
        copies[3 + o].wait_recv()
    total = land2[0]
    for z in range(1, N_ROW):
        total = total + land2[z]
    strip = pl.multiple_of(col * 64 + rep * 16, 16)
    spot = (
        pl.ds(pl.multiple_of(strip + 8 * (mine // 4), 8), 8),
        pl.ds(pl.multiple_of(128 * lax.rem(mine, 4), 128), 128),
    )
    out_ref[spot] = total
    gather = []
    for i, o in enumerate((1, 2, 3, -1, -2, -3, -4)):
        peer = {"row": lax.rem(row + N_ROW + o, N_ROW)}
        copy = remote(out_ref.at[spot], out_ref.at[spot], s3.at[i], r3.at[i], peer)
        copy.start()
        gather.append(copy)
    for copy in gather:
        copy.wait()

    here = out_ref.at[pl.ds(strip, 16)]
    spread = []
    for i, peer in enumerate(plane):
        copy = remote(here, here, s4.at[i], r4.at[i], peer)
        copy.start()
        spread.append(copy)
    passed = remote(here, here, s5.at[15], r5.at[15], sibling)
    passed.start()
    onward = [passed]
    for h in range(2):
        for o in range(N_COL):
            if h or o:
                i = h * N_COL + o - 1
                start = lax.rem(col + N_COL - o, N_COL) * 64 + (lax.rem(half + h, 2) * 2 + core) * 16
                there = out_ref.at[pl.ds(pl.multiple_of(start, 16), 16)]
                spread[i].wait_recv()
                copy = remote(there, there, s5.at[i], r5.at[i], sibling)
                copy.start()
                onward.append(copy)
    for copy in copies + spread:
        copy.wait_send()
    for copy in onward:
        copy.wait()


def sum_gram(x):
    dma = pltpu.SemaphoreType.DMA
    sems = [dma((n,)) for n in (3, 3, 15, 15, 7, 7, 15, 15, 16, 16)]
    return pl.pallas_call(
        gram_kernel,
        out_shape=jax.ShapeDtypeStruct((x.shape[1], x.shape[1]), F32),
        in_specs=[pl.BlockSpec(memory_space=pltpu.VMEM)],
        out_specs=pl.BlockSpec(memory_space=pltpu.VMEM),
        scratch_shapes=[
            pltpu.VMEM((3, 16, 512), F32),
            pltpu.VMEM((8, 8, 128), F32),
            pltpu.VMEM((16, 8, 128), F32),
        ]
        + sems,
        compiler_params=pltpu.CompilerParams(collective_id=2, has_side_effects=True, vmem_limit_bytes=32 << 20),
        name="sum_gram",
    )(x)


def factor_kernel(x_ref, out_ref, land1, part, land2, s1, r1, s2, r2, s3, r3):
    row, rep = lax.axis_index("row"), lax.axis_index("rep")
    rep_peers = others("rep", N_REP)
    row_peers = others("row", N_ROW)
    greet(rep_peers + row_peers)
    rank, wide = x_ref.shape
    wide = wide // N_REP
    rank = rank // N_ROW
    copies = []
    for o, peer in enumerate(rep_peers):
        start = pl.multiple_of(peer["rep"] * wide, wide)
        copy = remote(x_ref.at[:, pl.ds(start, wide)], land1.at[o], s1.at[o], r1.at[o], peer)
        copy.start()
        copies.append(copy)
    mine = pl.ds(pl.multiple_of(rep * wide, wide), wide)
    for o in range(N_REP - 1):
        copies[o].wait_recv()

    def add(i, carry):
        here = pl.ds(pl.multiple_of(i * rank, rank), rank)
        total = x_ref[here, mine].astype(F32)
        for o in range(N_REP - 1):
            total = total + land1[o, here].astype(F32)
        part[i] = total.astype(BF16)
        return carry

    lax.fori_loop(0, N_ROW, add, 0)
    for o, peer in enumerate(row_peers):
        copy = remote(part.at[peer["row"]], land2.at[o], s2.at[o], r2.at[o], peer)
        copy.start()
        copies.append(copy)
    total = part[row].astype(F32)
    for o in range(N_ROW - 1):
        copies[N_REP - 1 + o].wait_recv()
        total = total + land2[o].astype(F32)
    out_ref[:, mine] = total
    for o, peer in enumerate(rep_peers):
        copy = remote(out_ref.at[:, mine], out_ref.at[:, mine], s3.at[o], r3.at[o], peer)
        copy.start()
        copy_out = copy
        copies.append(copy_out)
    for copy in copies[N_REP - 1 + N_ROW - 1 :]:
        copy.wait_recv()
    for copy in copies:
        copy.wait_send()


def sum_factor(x):
    dma = pltpu.SemaphoreType.DMA
    rank, wide = x.shape[0] // N_ROW, x.shape[1] // N_REP
    return pl.pallas_call(
        factor_kernel,
        out_shape=jax.ShapeDtypeStruct((rank, x.shape[1]), F32),
        in_specs=[pl.BlockSpec(memory_space=pltpu.VMEM)],
        out_specs=pl.BlockSpec(memory_space=pltpu.VMEM),
        scratch_shapes=[
            pltpu.VMEM((N_REP - 1, x.shape[0], wide), BF16),
            pltpu.VMEM((N_ROW, rank, wide), BF16),
            pltpu.VMEM((N_ROW - 1, rank, wide), BF16),
        ]
        + [dma((n,)) for n in (3, 3, 15, 15, 3, 3)],
        compiler_params=pltpu.CompilerParams(collective_id=3, has_side_effects=True, vmem_limit_bytes=32 << 20),
        name="sum_factor",
    )(x)


def shards(tokens, out_grad, moment_old, basis_old, factor_old, test_matrix):
    activations = lax.all_gather(tokens[0], "col", axis=0, tiled=True)
    upstream = lax.all_gather(out_grad[0], "row", axis=0, tiled=True)
    partial_value = lax.dot_general(
        activations, upstream, (((0,), (0,)), ((), ())), preferred_element_type=jnp.float32
    )
    partial_value = lax.optimization_barrier(partial_value.astype(jnp.bfloat16))
    gradient = lax.psum_scatter(
        partial_value.astype(jnp.float32).astype(jnp.bfloat16),
        "rep",
        scatter_dimension=0,
        tiled=True,
    ).astype(jnp.float32)
    moment = 0.9 * moment_old + 0.1 * gradient
    previous = jnp.dot(
        basis_old,
        lax.all_gather(factor_old, "row", axis=1, tiled=True).T,
        precision=lax.Precision.HIGHEST,
    )
    second = (0.95 * previous + 0.05 * gradient * gradient).astype(jnp.bfloat16)
    sketch = sum_sketch(jnp.dot(second, test_matrix, preferred_element_type=jnp.float32))
    rank_full = sketch.shape[1]
    block = rank_full // N_COL
    own = lax.dynamic_slice_in_dim(sketch, lax.axis_index("col") * block, block, 1)
    gram_matrix = sum_gram(jnp.dot(own.T, sketch, precision=lax.Precision.HIGHEST))
    ridge_shift = 0.01 * jnp.trace(gram_matrix) / rank_full
    lower_factor = jnp.linalg.cholesky(
        gram_matrix + ridge_shift * jnp.eye(rank_full, dtype=jnp.float32)
    )
    orthonormal = jax.scipy.linalg.solve_triangular(lower_factor, sketch.T, lower=True).T
    basis_bf = orthonormal.astype(jnp.bfloat16)
    product = lax.dot_general(
        basis_bf, second, (((0,), (0,)), ((), ())), preferred_element_type=jnp.float32
    )
    factor_new = sum_factor(product.astype(BF16)).T
    return (moment, orthonormal, factor_new)


def solution(mesh):
    placed = (
        P("rep", "col", "row"),
        P("rep", "row", "col"),
        P(("row", "rep"), "col"),
        P(("row", "rep"), None),
        P("col", "row"),
        P("col", None),
    )
    return jax.shard_map(
        shards,
        mesh=mesh,
        in_specs=placed,
        out_specs=(P(("row", "rep"), "col"), P(("row", "rep"), None), P("col", "row")),
        check_vma=False,
    )
```

```python
import functools

import jax
import jax.numpy as jnp
from jax import lax
from jax.experimental import pallas as pl
from jax.experimental.pallas import tpu as pltpu
from jax.sharding import PartitionSpec as P

MESH = pl.DeviceIdType.MESH
F32 = jnp.float32
BF16 = jnp.bfloat16
N_ROW, N_COL, N_REP = 16, 8, 4


def remote(src, dst, send, recv, device):
    return pltpu.make_async_remote_copy(
        src_ref=src, dst_ref=dst, send_sem=send, recv_sem=recv, device_id=device, device_id_type=MESH
    )


def greet(devices):
    barrier = pltpu.get_barrier_semaphore()
    for device in devices:
        pl.semaphore_signal(barrier, inc=1, device_id=device, device_id_type=MESH)
    pl.semaphore_wait(barrier, len(devices))


def others(axis, size):
    me = lax.axis_index(axis)
    return [{axis: lax.rem(me + o, size)} for o in range(1, size)]


def sketch_kernel(x_ref, out_ref, landed, send1, recv1, send2, recv2):
    me = lax.axis_index("col")
    peers = others("col", N_COL)
    greet(peers)
    rows = x_ref.shape[0] // N_COL
    first = []
    for o, peer in enumerate(peers):
        start = pl.multiple_of(peer["col"] * rows, rows)
        copy = remote(x_ref.at[pl.ds(start, rows)], landed.at[o], send1.at[o], recv1.at[o], peer)
        copy.start()
        first.append(copy)
    mine = pl.ds(pl.multiple_of(me * rows, rows), rows)
    total = x_ref[mine]
    for o in range(N_COL - 1):
        first[o].wait_recv()
        total = total + landed[o]
    out_ref[mine] = total
    second = []
    for o, peer in enumerate(peers):
        copy = remote(out_ref.at[mine], out_ref.at[mine], send2.at[o], recv2.at[o], peer)
        copy.start()
        second.append(copy)
    for copy in first:
        copy.wait_send()
    for copy in second:
        copy.wait()


def sum_sketch(x):
    rows = x.shape[0] // N_COL
    n = N_COL - 1
    return pl.pallas_call(
        sketch_kernel,
        out_shape=jax.ShapeDtypeStruct(x.shape, F32),
        in_specs=[pl.BlockSpec(memory_space=pltpu.VMEM)],
        out_specs=pl.BlockSpec(memory_space=pltpu.VMEM),
        scratch_shapes=[pltpu.VMEM((n, rows, x.shape[1]), F32)] + [pltpu.SemaphoreType.DMA((n,))] * 4,
        compiler_params=pltpu.CompilerParams(collective_id=1, has_side_effects=True, vmem_limit_bytes=32 << 20),
        name="sum_sketch",
    )(x)


def gram_kernel(x_ref, out_ref, land1, tiles, land2, s1, r1, s2, r2, s3, r3, s4, r4, s5, r5):
    row, col, rep = lax.axis_index("row"), lax.axis_index("col"), lax.axis_index("rep")
    half, core = rep // 2, lax.rem(rep, 2)
    rep_peers = others("rep", N_REP)
    row_peers = others("row", N_ROW)
    plane = []
    for h in range(2):
        for o in range(N_COL):
            if h or o:
                plane.append({"col": lax.rem(col + o, N_COL), "rep": lax.rem(half + h, 2) * 2 + core})
    sibling = {"rep": half * 2 + 1 - core}
    greet(rep_peers + row_peers + plane)

    copies = []
    for o, peer in enumerate(rep_peers):
        start = pl.multiple_of(peer["rep"] * 16, 16)
        copy = remote(x_ref.at[pl.ds(start, 16)], land1.at[o], s1.at[o], r1.at[o], peer)
        copy.start()
        copies.append(copy)
    total = x_ref[pl.ds(pl.multiple_of(rep * 16, 16), 16)]
    for o in range(N_REP - 1):
        copies[o].wait_recv()
        total = total + land1[o]
    for t in range(8):
        tiles[t] = total[8 * (t // 4) : 8 * (t // 4) + 8, 128 * (t % 4) : 128 * (t % 4) + 128]

    mine = lax.rem(row, 8)
    for o, peer in enumerate(row_peers):
        copy = remote(tiles.at[lax.rem(peer["row"], 8)], land2.at[row], s2.at[o], r2.at[o], peer)
        copy.start()
        copies.append(copy)
    land2[row] = tiles[mine]
    for o in range(N_ROW - 1):
        copies[3 + o].wait_recv()
    total = land2[0]
    for z in range(1, N_ROW):
        total = total + land2[z]
    strip = pl.multiple_of(col * 64 + rep * 16, 16)
    spot = (
        pl.ds(pl.multiple_of(strip + 8 * (mine // 4), 8), 8),
        pl.ds(pl.multiple_of(128 * lax.rem(mine, 4), 128), 128),
    )
    out_ref[spot] = total
    gather = []
    for i, o in enumerate((1, 2, 3, -1, -2, -3, -4)):
        peer = {"row": lax.rem(row + N_ROW + o, N_ROW)}
        copy = remote(out_ref.at[spot], out_ref.at[spot], s3.at[i], r3.at[i], peer)
        copy.start()
        gather.append(copy)
    for copy in gather:
        copy.wait()

    here = out_ref.at[pl.ds(strip, 16)]
    spread = []
    for i, peer in enumerate(plane):
        copy = remote(here, here, s4.at[i], r4.at[i], peer)
        copy.start()
        spread.append(copy)
    passed = remote(here, here, s5.at[15], r5.at[15], sibling)
    passed.start()
    onward = [passed]
    for h in range(2):
        for o in range(N_COL):
            if h or o:
                i = h * N_COL + o - 1
                start = lax.rem(col + N_COL - o, N_COL) * 64 + (lax.rem(half + h, 2) * 2 + core) * 16
                there = out_ref.at[pl.ds(pl.multiple_of(start, 16), 16)]
                spread[i].wait_recv()
                copy = remote(there, there, s5.at[i], r5.at[i], sibling)
                copy.start()
                onward.append(copy)
    for copy in copies + spread:
        copy.wait_send()
    for copy in onward:
        copy.wait()


def sum_gram(x):
    dma = pltpu.SemaphoreType.DMA
    sems = [dma((n,)) for n in (3, 3, 15, 15, 7, 7, 15, 15, 16, 16)]
    return pl.pallas_call(
        gram_kernel,
        out_shape=jax.ShapeDtypeStruct((x.shape[1], x.shape[1]), F32),
        in_specs=[pl.BlockSpec(memory_space=pltpu.VMEM)],
        out_specs=pl.BlockSpec(memory_space=pltpu.VMEM),
        scratch_shapes=[
            pltpu.VMEM((3, 16, 512), F32),
            pltpu.VMEM((8, 8, 128), F32),
            pltpu.VMEM((16, 8, 128), F32),
        ]
        + sems,
        compiler_params=pltpu.CompilerParams(collective_id=2, has_side_effects=True, vmem_limit_bytes=32 << 20),
        name="sum_gram",
    )(x)


def factor_kernel(x_ref, out_ref, land1, part, land2, s1, r1, s2, r2, s3, r3):
    row, rep = lax.axis_index("row"), lax.axis_index("rep")
    rep_peers = others("rep", N_REP)
    row_peers = others("row", N_ROW)
    greet(rep_peers + row_peers)
    rank, wide = x_ref.shape
    wide = wide // N_REP
    rank = rank // N_ROW
    copies = []
    for o, peer in enumerate(rep_peers):
        start = pl.multiple_of(peer["rep"] * wide, wide)
        copy = remote(x_ref.at[:, pl.ds(start, wide)], land1.at[o], s1.at[o], r1.at[o], peer)
        copy.start()
        copies.append(copy)
    mine = pl.ds(pl.multiple_of(rep * wide, wide), wide)
    for o in range(N_REP - 1):
        copies[o].wait_recv()

    def add(i, carry):
        here = pl.ds(pl.multiple_of(i * rank, rank), rank)
        total = x_ref[here, mine].astype(F32)
        for o in range(N_REP - 1):
            total = total + land1[o, here].astype(F32)
        part[i] = total.astype(BF16)
        return carry

    lax.fori_loop(0, N_ROW, add, 0)
    for o, peer in enumerate(row_peers):
        copy = remote(part.at[peer["row"]], land2.at[o], s2.at[o], r2.at[o], peer)
        copy.start()
        copies.append(copy)
    total = part[row].astype(F32)
    for o in range(N_ROW - 1):
        copies[N_REP - 1 + o].wait_recv()
        total = total + land2[o].astype(F32)
    out_ref[:, mine] = total
    for o, peer in enumerate(rep_peers):
        copy = remote(out_ref.at[:, mine], out_ref.at[:, mine], s3.at[o], r3.at[o], peer)
        copy.start()
        copy_out = copy
        copies.append(copy_out)
    for copy in copies[N_REP - 1 + N_ROW - 1 :]:
        copy.wait_recv()
    for copy in copies:
        copy.wait_send()


def sum_factor(x):
    dma = pltpu.SemaphoreType.DMA
    rank, wide = x.shape[0] // N_ROW, x.shape[1] // N_REP
    return pl.pallas_call(
        factor_kernel,
        out_shape=jax.ShapeDtypeStruct((rank, x.shape[1]), F32),
        in_specs=[pl.BlockSpec(memory_space=pltpu.VMEM)],
        out_specs=pl.BlockSpec(memory_space=pltpu.VMEM),
        scratch_shapes=[
            pltpu.VMEM((N_REP - 1, x.shape[0], wide), BF16),
            pltpu.VMEM((N_ROW, rank, wide), BF16),
            pltpu.VMEM((N_ROW - 1, rank, wide), BF16),
        ]
        + [dma((n,)) for n in (3, 3, 15, 15, 3, 3)],
        compiler_params=pltpu.CompilerParams(collective_id=3, has_side_effects=True, vmem_limit_bytes=32 << 20),
        name="sum_factor",
    )(x)


def gather_kernel(tok_ref, og_ref, fa_ref, tk_ref, g_ref, f_ref, rs, rr, ss, sr, xs, xr, ts, tr, cs, cr):
    row, col, rep = lax.axis_index("row"), lax.axis_index("col"), lax.axis_index("rep")
    half, core = rep // 2, lax.rem(rep, 2)
    across = (1 - half) * 2 + core
    sibling = half * 2 + 1 - core
    rep_peers = others("rep", N_REP)
    col_peers = others("col", N_COL)
    sides = ({"row": lax.rem(row + 1, N_ROW)}, {"row": lax.rem(row + N_ROW - 1, N_ROW)})
    wide = tok_ref.shape[1] // N_REP
    part = pl.ds(pl.multiple_of(rep * wide, wide), wide)
    g_ref[rep, row] = og_ref[...]
    f_ref[row, 0] = fa_ref[:16]
    f_ref[row, 1] = fa_ref[16:]
    tk_ref[col, rep] = tok_ref[:, part]
    greet(rep_peers + col_peers + list(sides))

    def slot(stream, z, c=core):
        if stream == 2:
            return f_ref.at[z, c]
        return g_ref.at[(half if stream == 0 else 1 - half) * 2 + c, z]

    def ring(stream, side, step):
        z = lax.rem(row + N_ROW + (1 - step if side == 0 else step - 1), N_ROW)
        return remote(slot(stream, z), slot(stream, z), rs.at[stream, side, step], rr.at[stream, side, step], sides[side])

    def arrival(stream, side, step):
        z = lax.rem(row + N_ROW + (-step if side == 0 else step), N_ROW)
        return remote(slot(stream, z), slot(stream, z), rs.at[stream, side, step], rr.at[stream, side, step], sides[side])

    def hand(stream, index, c=core):
        z = lax.rem(row + N_ROW + jnp.where(index <= 8, -index, index - 8), N_ROW)
        return remote(slot(stream, z, c), slot(stream, z, c), ss.at[stream, index], sr.at[stream, index], {"rep": sibling})

    swap = remote(slot(0, row), slot(0, row), xs, xr, {"rep": across})
    swap.start()
    for stream in (0, 2):
        for side in range(2):
            ring(stream, side, 1).start()
    first = []
    for o, peer in enumerate(rep_peers):
        start = pl.multiple_of(peer["rep"] * wide, wide)
        copy = remote(tok_ref.at[:, pl.ds(start, wide)], tk_ref.at[col, rep], ts.at[o], tr.at[o], peer)
        copy.start()
        first.append(copy)
    hand(0, 0).start()
    swap.wait_recv()
    for side in range(2):
        ring(1, side, 1).start()
    hand(1, 0).start()
    for copy in first:
        copy.wait_recv()
    second = []
    for o, peer in enumerate(col_peers):
        copy = remote(tk_ref.at[col], tk_ref.at[col], cs.at[o], cr.at[o], peer)
        copy.start()
        second.append(copy)

    def step(s, carry):
        for stream in (0, 2, 1):
            arrival(stream, 0, s).wait_recv()
            ring(stream, 0, s + 1).start()
            hand(stream, s).start()
            arrival(stream, 1, s).wait_recv()

            @pl.when(s < 7)
            def _():
                ring(stream, 1, s + 1).start()

            hand(stream, s + 8).start()
        return carry

    lax.fori_loop(1, 8, step, 0)
    for stream in (0, 2, 1):
        arrival(stream, 0, 8).wait_recv()
        hand(stream, 8).start()
    for copy in second:
        copy.wait_recv()

    def finish(i, carry):
        for stream in range(3):
            hand(stream, i, 1 - core).wait_recv()
            hand(stream, i).wait_send()
        return carry

    for stream in range(2):
        hand(stream, 0, 1 - core).wait_recv()
        hand(stream, 0).wait_send()
    lax.fori_loop(1, 16, finish, 0)

    def drain(s, carry):
        for stream in range(3):
            for side in range(2):
                ring(stream, side, s).wait_send()
        return carry

    lax.fori_loop(1, 8, drain, 0)
    for stream in range(3):
        ring(stream, 0, 8).wait_send()
    swap.wait_send()
    for copy in first + second:
        copy.wait_send()


def gather(tokens, out_grad, factor):
    dma = pltpu.SemaphoreType.DMA
    vmem = pl.BlockSpec(memory_space=pltpu.VMEM)
    depth, wide = tokens.shape[0], tokens.shape[1] // N_REP
    tall, across = out_grad.shape
    return pl.pallas_call(
        gather_kernel,
        out_shape=(
            jax.ShapeDtypeStruct((N_COL, N_REP, depth, wide), BF16),
            jax.ShapeDtypeStruct((N_REP, N_ROW, tall, across), BF16),
            jax.ShapeDtypeStruct((N_ROW, 2, factor.shape[0] // 2, across), BF16),
        ),
        in_specs=[vmem] * 3,
        out_specs=(vmem,) * 3,
        scratch_shapes=[
            dma((3, 2, 9)), dma((3, 2, 9)), dma((3, 16)), dma((3, 16)), dma, dma,
            dma((3,)), dma((3,)), dma((7,)), dma((7,)),
        ],
        compiler_params=pltpu.CompilerParams(collective_id=4, has_side_effects=True, vmem_limit_bytes=32 << 20),
        name="gather",
    )(tokens, out_grad, factor)


def tile_kernel(tk_ref, g_ref, f_ref, moment_ref, basis_ref, test_ref, new_ref, second_ref, part_ref, high, low):
    step = 256
    high[...] = basis_ref[...].astype(BF16)
    low[...] = (basis_ref[...] - high[...].astype(F32)).astype(BF16)
    rank = basis_ref.shape[1]
    part_ref[...] = jnp.zeros_like(part_ref)

    def columns(i, carry):
        here = pl.ds(pl.multiple_of(i * step, step), step)
        gradient = jnp.zeros((new_ref.shape[0], step), F32)
        for b in range(N_REP):
            left = tk_ref[:, b].reshape(-1, tk_ref.shape[3])
            right = g_ref[b, :, :, here].reshape(-1, step)
            piece = lax.dot_general(left, right, (((0,), (0,)), ((), ())), preferred_element_type=F32)
            gradient = gradient + piece.astype(BF16).astype(F32)
        new_ref[:, here] = 0.9 * moment_ref[:, here] + 0.1 * gradient
        factor = f_ref[:, :, :, here].reshape(rank, step)
        previous = jnp.dot(high[...], factor, preferred_element_type=F32)
        previous = previous + jnp.dot(low[...], factor, preferred_element_type=F32)
        second = (0.95 * previous + 0.05 * gradient * gradient).astype(BF16)
        second_ref[:, here] = second
        part_ref[...] += jnp.dot(second, test_ref[here], preferred_element_type=F32)
        return carry

    lax.fori_loop(0, new_ref.shape[1] // step, columns, 0)


def tile(tk, g, f, moment_old, basis_old, test_matrix):
    vmem = pl.BlockSpec(memory_space=pltpu.VMEM)
    rows, columns = moment_old.shape
    rank = basis_old.shape[1]
    return pl.pallas_call(
        tile_kernel,
        out_shape=(
            jax.ShapeDtypeStruct((rows, columns), F32),
            jax.ShapeDtypeStruct((rows, columns), BF16),
            jax.ShapeDtypeStruct((rows, rank), F32),
        ),
        in_specs=[vmem] * 6,
        out_specs=(vmem,) * 3,
        scratch_shapes=[pltpu.VMEM((rows, rank), BF16)] * 2,
        compiler_params=pltpu.CompilerParams(vmem_limit_bytes=32 << 20),
        name="tile",
    )(tk, g, f, moment_old, basis_old, test_matrix)


SPAN = 128


def invert_diagonal(block):
    count = SPAN // 8
    d = [block[8 * i : 8 * i + 8, :] for i in range(count)]
    lane = lax.broadcasted_iota(jnp.int32, (8, SPAN), 1)
    sub = lax.broadcasted_iota(jnp.int32, (8, SPAN), 0)
    x = [jnp.where(lane == sub + 8 * i, 1.0, 0.0).astype(F32) for i in range(count)]
    out = []

    def spread(value):
        return jnp.broadcast_to(value, (8, SPAN))

    for b0 in range(count):
        j0 = 8 * b0
        rows, extra = d[b0], x[b0]
        wide = [spread(rows[:, j0 + m : j0 + m + 1]) for m in range(8)]
        s = [[spread(wide[m][i : i + 1, :]) if m <= i else None for m in range(8)] for i in range(8)]
        p = [spread(rows[i : i + 1, :]) for i in range(8)]
        q = [spread(extra[i : i + 1, :]) for i in range(8)]
        inverse = [None] * 8
        f = [[None] * 8 for _ in range(8)]
        for m in range(8):
            inverse[m] = 1.0 / s[m][m]
            for i in range(m + 1, 8):
                f[i][m] = s[i][m] * inverse[m]
            for i in range(m + 1, 8):
                for l in range(m + 1, i + 1):
                    s[i][l] = s[i][l] - f[i][m] * s[l][m]
            for i in range(m + 1, 8):
                p[i] = p[i] - f[i][m] * p[m]
                q[i] = q[i] - f[i][m] * q[m]
        done = jnp.zeros((8, SPAN), F32)
        for i in range(8):
            done = jnp.where(sub == i, q[i] * lax.rsqrt(s[i][i]), done)
        out.append(done)
        v, w = [None] * 8, [None] * 8
        for i in reversed(range(8)):
            v[i] = p[i] * inverse[i]
            w[i] = q[i] * inverse[i]
            for m in range(i + 1, 8):
                v[i] = v[i] - f[m][i] * v[m]
                w[i] = w[i] - f[m][i] * w[m]
        for b in range(b0 + 1, count):
            source, left, right = d[b], d[b], x[b]
            for m in range(8):
                c = spread(source[:, j0 + m : j0 + m + 1])
                left = left - c * v[m]
                right = right - c * w[m]
            d[b], x[b] = left, right
    return jnp.concatenate(out, 0)


def exact(a, b, dims):
    return lax.dot_general(a, b, (dims, ((), ())), precision=lax.Precision.HIGHEST, preferred_element_type=F32)


def inverse_kernel(g_ref, m_ref, a):
    n = g_ref.shape[0]
    eye = lax.broadcasted_iota(jnp.int32, (n, n), 0) == lax.broadcasted_iota(jnp.int32, (n, n), 1)
    gram = g_ref[...]
    shift = 0.01 * jnp.sum(jnp.where(eye, gram, 0.0)) / n
    a[...] = jnp.where(eye, gram + shift, gram)
    m_ref[...] = jnp.where(eye, 1.0, 0.0).astype(F32)
    for k in range(n // SPAN):
        end = (k + 1) * SPAN
        own, rest = slice(k * SPAN, end), slice(end, n)
        inverse = invert_diagonal(a[own, own])
        rows = exact(inverse, m_ref[own, :end], ((1,), (0,)))
        m_ref[own, :end] = rows
        if end < n:
            panel = exact(a[rest, own], inverse, ((1,), (1,)))
            a[rest, rest] = a[rest, rest] - exact(panel, panel, ((1,), (1,)))
            m_ref[rest, :end] = m_ref[rest, :end] - exact(panel, rows, ((1,), (0,)))


def inverse_factor(gram):
    vmem = pl.BlockSpec(memory_space=pltpu.VMEM)
    return pl.pallas_call(
        inverse_kernel,
        out_shape=jax.ShapeDtypeStruct(gram.shape, F32),
        in_specs=[vmem],
        out_specs=vmem,
        scratch_shapes=[pltpu.VMEM(gram.shape, F32)],
        compiler_params=pltpu.CompilerParams(vmem_limit_bytes=32 << 20),
        name="inverse_factor",
    )(gram)


def shards(tokens, out_grad, moment_old, basis_old, factor_old, test_matrix):
    tk, g, f = gather(tokens[0], out_grad[0], factor_old.T.astype(BF16))
    moment, second, part = tile(tk, g, f, moment_old, basis_old, test_matrix)
    sketch = sum_sketch(part)
    block = sketch.shape[1] // N_COL
    own = lax.dynamic_slice_in_dim(sketch, lax.axis_index("col") * block, block, 1)
    gram_matrix = sum_gram(jnp.dot(own.T, sketch, precision=lax.Precision.HIGHEST))
    inverse = inverse_factor(gram_matrix)
    orthonormal = jnp.dot(sketch, inverse.T, precision=lax.Precision.HIGHEST)
    basis_bf = orthonormal.astype(jnp.bfloat16)
    product = lax.dot_general(
        basis_bf, second, (((0,), (0,)), ((), ())), preferred_element_type=jnp.float32
    )
    factor_new = sum_factor(product.astype(BF16)).T
    return (moment, orthonormal, factor_new)


def solution(mesh):
    placed = (
        P("rep", "col", "row"),
        P("rep", "row", "col"),
        P(("row", "rep"), "col"),
        P(("row", "rep"), None),
        P("col", "row"),
        P("col", None),
    )
    return jax.shard_map(
        shards,
        mesh=mesh,
        in_specs=placed,
        out_specs=(P(("row", "rep"), "col"), P(("row", "rep"), None), P("col", "row")),
        check_vma=False,
    )
```

```python
import functools

import jax
import jax.numpy as jnp
from jax import lax
from jax.experimental import pallas as pl
from jax.experimental.pallas import tpu as pltpu
from jax.sharding import PartitionSpec as P

MESH = pl.DeviceIdType.MESH
F32 = jnp.float32
BF16 = jnp.bfloat16
N_ROW, N_COL, N_REP = 16, 8, 4


def remote(src, dst, send, recv, device):
    return pltpu.make_async_remote_copy(
        src_ref=src, dst_ref=dst, send_sem=send, recv_sem=recv, device_id=device, device_id_type=MESH
    )


def greet(devices):
    barrier = pltpu.get_barrier_semaphore()
    for device in devices:
        pl.semaphore_signal(barrier, inc=1, device_id=device, device_id_type=MESH)
    pl.semaphore_wait(barrier, len(devices))


def others(axis, size):
    me = lax.axis_index(axis)
    return [{axis: lax.rem(me + o, size)} for o in range(1, size)]


def gather_kernel(tok_ref, og_ref, fa_ref, tk_ref, g_ref, f_ref, rs, rr, ss, sr, xs, xr, ts, tr, cs, cr):
    row, col, rep = lax.axis_index("row"), lax.axis_index("col"), lax.axis_index("rep")
    half, core = rep // 2, lax.rem(rep, 2)
    across = (1 - half) * 2 + core
    sibling = half * 2 + 1 - core
    rep_peers = others("rep", N_REP)
    col_peers = others("col", N_COL)
    sides = ({"row": lax.rem(row + 1, N_ROW)}, {"row": lax.rem(row + N_ROW - 1, N_ROW)})
    wide = tok_ref.shape[1] // N_REP
    part = pl.ds(pl.multiple_of(rep * wide, wide), wide)
    g_ref[rep, row] = og_ref[...]
    f_ref[row, 0] = fa_ref[:16]
    f_ref[row, 1] = fa_ref[16:]
    tk_ref[col, rep] = tok_ref[:, part]
    greet(rep_peers + col_peers + list(sides))

    def slot(stream, z, c=core):
        if stream == 2:
            return f_ref.at[z, c]
        return g_ref.at[(half if stream == 0 else 1 - half) * 2 + c, z]

    def ring(stream, side, step):
        z = lax.rem(row + N_ROW + (1 - step if side == 0 else step - 1), N_ROW)
        return remote(slot(stream, z), slot(stream, z), rs.at[stream, side, step], rr.at[stream, side, step], sides[side])

    def arrival(stream, side, step):
        z = lax.rem(row + N_ROW + (-step if side == 0 else step), N_ROW)
        return remote(slot(stream, z), slot(stream, z), rs.at[stream, side, step], rr.at[stream, side, step], sides[side])

    def hand(stream, index, c=core):
        z = lax.rem(row + N_ROW + jnp.where(index <= 8, -index, index - 8), N_ROW)
        return remote(slot(stream, z, c), slot(stream, z, c), ss.at[stream, index], sr.at[stream, index], {"rep": sibling})

    swap = remote(slot(0, row), slot(0, row), xs, xr, {"rep": across})
    swap.start()
    for stream in (0, 2):
        for side in range(2):
            ring(stream, side, 1).start()
    first = []
    for o, peer in enumerate(rep_peers):
        start = pl.multiple_of(peer["rep"] * wide, wide)
        copy = remote(tok_ref.at[:, pl.ds(start, wide)], tk_ref.at[col, rep], ts.at[o], tr.at[o], peer)
        copy.start()
        first.append(copy)
    hand(0, 0).start()
    swap.wait_recv()
    for side in range(2):
        ring(1, side, 1).start()
    hand(1, 0).start()
    for copy in first:
        copy.wait_recv()
    second = []
    for o, peer in enumerate(col_peers):
        copy = remote(tk_ref.at[col], tk_ref.at[col], cs.at[o], cr.at[o], peer)
        copy.start()
        second.append(copy)

    def step(s, carry):
        for stream in (0, 2, 1):
            arrival(stream, 0, s).wait_recv()
            ring(stream, 0, s + 1).start()
            hand(stream, s).start()
            arrival(stream, 1, s).wait_recv()

            @pl.when(s < 7)
            def _():
                ring(stream, 1, s + 1).start()

            hand(stream, s + 8).start()
        return carry

    lax.fori_loop(1, 8, step, 0)
    for stream in (0, 2, 1):
        arrival(stream, 0, 8).wait_recv()
        hand(stream, 8).start()
    for copy in second:
        copy.wait_recv()

    def finish(i, carry):
        for stream in range(3):
            hand(stream, i, 1 - core).wait_recv()
            hand(stream, i).wait_send()
        return carry

    for stream in range(2):
        hand(stream, 0, 1 - core).wait_recv()
        hand(stream, 0).wait_send()
    lax.fori_loop(1, 16, finish, 0)

    def drain(s, carry):
        for stream in range(3):
            for side in range(2):
                ring(stream, side, s).wait_send()
        return carry

    lax.fori_loop(1, 8, drain, 0)
    for stream in range(3):
        ring(stream, 0, 8).wait_send()
    swap.wait_send()
    for copy in first + second:
        copy.wait_send()


def gather(tokens, out_grad, factor):
    dma = pltpu.SemaphoreType.DMA
    vmem = pl.BlockSpec(memory_space=pltpu.VMEM)
    depth, wide = tokens.shape[0], tokens.shape[1] // N_REP
    tall, across = out_grad.shape
    return pl.pallas_call(
        gather_kernel,
        out_shape=(
            jax.ShapeDtypeStruct((N_COL, N_REP, depth, wide), BF16),
            jax.ShapeDtypeStruct((N_REP, N_ROW, tall, across), BF16),
            jax.ShapeDtypeStruct((N_ROW, 2, factor.shape[0] // 2, across), BF16),
        ),
        in_specs=[vmem] * 3,
        out_specs=(vmem,) * 3,
        scratch_shapes=[
            dma((3, 2, 9)), dma((3, 2, 9)), dma((3, 16)), dma((3, 16)), dma, dma,
            dma((3,)), dma((3,)), dma((7,)), dma((7,)),
        ],
        compiler_params=pltpu.CompilerParams(collective_id=4, has_side_effects=True, vmem_limit_bytes=12 << 20),
        name="gather",
    )(tokens, out_grad, factor)


def tile_kernel(tk_ref, g_ref, f_ref, moment_ref, basis_ref, test_ref, new_ref, second_ref, part_ref, high, low):
    step = 256
    high[...] = basis_ref[...].astype(BF16)
    low[...] = (basis_ref[...] - high[...].astype(F32)).astype(BF16)
    rank = basis_ref.shape[1]
    part_ref[...] = jnp.zeros_like(part_ref)

    def columns(i, carry):
        here = pl.ds(pl.multiple_of(i * step, step), step)
        gradient = jnp.zeros((new_ref.shape[0], step), F32)
        for b in range(N_REP):
            left = tk_ref[:, b].reshape(-1, tk_ref.shape[3])
            right = g_ref[b, :, :, here].reshape(-1, step)
            piece = lax.dot_general(left, right, (((0,), (0,)), ((), ())), preferred_element_type=F32)
            gradient = gradient + piece.astype(BF16).astype(F32)
        new_ref[:, here] = 0.9 * moment_ref[:, here] + 0.1 * gradient
        factor = f_ref[:, :, :, here].reshape(rank, step)
        previous = jnp.dot(high[...], factor, preferred_element_type=F32)
        previous = previous + jnp.dot(low[...], factor, preferred_element_type=F32)
        second = (0.95 * previous + 0.05 * gradient * gradient).astype(BF16)
        second_ref[:, here] = second
        part_ref[...] += jnp.dot(second, test_ref[here], preferred_element_type=F32)
        return carry

    lax.fori_loop(0, new_ref.shape[1] // step, columns, 0)


def tile(tk, g, f, moment_old, basis_old, test_matrix):
    vmem = pl.BlockSpec(memory_space=pltpu.VMEM)
    rows, columns = moment_old.shape
    rank = basis_old.shape[1]
    return pl.pallas_call(
        tile_kernel,
        out_shape=(
            jax.ShapeDtypeStruct((rows, columns), F32),
            jax.ShapeDtypeStruct((rows, columns), BF16),
            jax.ShapeDtypeStruct((rows, rank), F32),
        ),
        in_specs=[vmem] * 6,
        out_specs=(vmem,) * 3,
        scratch_shapes=[pltpu.VMEM((rows, rank), BF16)] * 2,
        compiler_params=pltpu.CompilerParams(vmem_limit_bytes=20 << 20),
        name="tile",
    )(tk, g, f, moment_old, basis_old, test_matrix)


SPAN = 128


def invert_diagonal(block):
    sub = lax.broadcasted_iota(jnp.int32, (8, SPAN), 0)
    shape = (SPAN, SPAN)
    d = block
    x = (lax.broadcasted_iota(jnp.int32, shape, 0) == lax.broadcasted_iota(jnp.int32, shape, 1)).astype(F32)
    out = []

    def spread(value):
        return jnp.broadcast_to(value, (8, SPAN))

    for j0 in range(0, SPAN, 8):
        wide = [spread(d[:8, j0 + m : j0 + m + 1]) for m in range(8)]
        s = [[spread(wide[m][i : i + 1, :]) if m <= i else None for m in range(8)] for i in range(8)]
        p = [spread(d[i : i + 1, :]) for i in range(8)]
        q = [spread(x[i : i + 1, :]) for i in range(8)]
        inverse = [None] * 8
        f = [[None] * 8 for _ in range(8)]
        for m in range(8):
            inverse[m] = 1.0 / s[m][m]
            for i in range(m + 1, 8):
                f[i][m] = s[i][m] * inverse[m]
            for i in range(m + 1, 8):
                for l in range(m + 1, i + 1):
                    s[i][l] = s[i][l] - f[i][m] * s[l][m]
            for i in range(m + 1, 8):
                p[i] = p[i] - f[i][m] * p[m]
                q[i] = q[i] - f[i][m] * q[m]
        done = q[0] * lax.rsqrt(s[0][0])
        for i in range(1, 8):
            done = jnp.where(sub == i, q[i] * lax.rsqrt(s[i][i]), done)
        out.append(done)
        if j0 + 8 == SPAN:
            break
        v, w = [None] * 8, [None] * 8
        for i in reversed(range(8)):
            v[i] = p[i] * inverse[i]
            w[i] = q[i] * inverse[i]
            for m in range(i + 1, 8):
                v[i] = v[i] - f[m][i] * v[m]
                w[i] = w[i] - f[m][i] * w[m]
        d, x = d[8:], x[8:]
        source = d
        for m in range(8):
            c = source[:, j0 + m : j0 + m + 1]
            d = d - c * v[m][:1]
            x = x - c * w[m][:1]
    return jnp.concatenate(out, 0)


def exact(a, b, dims):
    return lax.dot_general(a, b, (dims, ((), ())), precision=lax.Precision.HIGHEST, preferred_element_type=F32)


def range_kernel(
    part_ref, second_ref, basis_ref, fac_ref,
    send_sk, land_sk, sk, gram, out, land1, tiles, land2, z, land_c, land_x, land_z, z_all, packed, m_ref, a_ref,
    s1, r1, s2, r2, s3, r3, s4, r4, s5, r5, s6, r6, s7, r7, zs1, zr1, zs2, zr2, zs3, zr3, zs4, zr4, fs, fr,
):
    row, col, rep = lax.axis_index("row"), lax.axis_index("col"), lax.axis_index("rep")
    half, core = rep // 2, lax.rem(rep, 2)
    rep_peers = others("rep", N_REP)
    row_peers = others("row", N_ROW)
    col_peers = others("col", N_COL)
    sibling = {"rep": half * 2 + 1 - core}
    across = {"rep": (1 - half) * 2 + core}
    plane = []
    for h in range(2):
        for o in range(N_COL):
            if h or o:
                plane.append({"col": lax.rem(col + o, N_COL), "rep": lax.rem(half + h, 2) * 2 + core})
    sends = []

    def start(src, dst, send, recv, device):
        copy = remote(src, dst, send, recv, device)
        copy.start()
        sends.append(copy)
        return copy

    send_sk[...] = part_ref[...].astype(BF16)
    greet(rep_peers + row_peers + plane)
    rows = part_ref.shape[0] // N_COL
    mine = pl.ds(pl.multiple_of(col * rows, rows), rows)
    copies = []
    for o, peer in enumerate(col_peers):
        there = pl.ds(pl.multiple_of(peer["col"] * rows, rows), rows)
        copies.append(start(send_sk.at[there], land_sk.at[o], s1.at[o], r1.at[o], peer))
    total = part_ref[mine]
    for o in range(N_COL - 1):
        copies[o].wait_recv()
        total = total + land_sk[o].astype(F32)
    sk[mine] = total.astype(BF16)
    copies = [start(sk.at[mine], sk.at[mine], s2.at[o], r2.at[o], peer) for o, peer in enumerate(col_peers)]
    for copy in copies:
        copy.wait_recv()

    sketch = sk[...]
    gram[...] = lax.dot_general(sketch, sketch, (((0,), (0,)), ((), ())), preferred_element_type=F32)
    copies = []
    for o, peer in enumerate(rep_peers):
        there = pl.ds(pl.multiple_of(col * 64 + peer["rep"] * 16, 16), 16)
        copies.append(start(gram.at[there], land1.at[o], s3.at[o], r3.at[o], peer))

    for i in range(4):
        piece = lax.dot_general(
            second_ref[:, 256 * i : 256 * i + 256], sketch, (((0,), (0,)), ((), ())), preferred_element_type=F32
        )
        z[4 * i : 4 * i + 4] = piece.reshape(4, N_REP, 16, sketch.shape[1])

    strip = pl.multiple_of(col * 64 + rep * 16, 16)
    total = gram[pl.ds(strip, 16)]
    for o in range(N_REP - 1):
        copies[o].wait_recv()
        total = total + land1[o]
    for t in range(8):
        tiles[t] = total[8 * (t // 4) : 8 * (t // 4) + 8, 128 * (t % 4) : 128 * (t % 4) + 128]
    tile_no = lax.rem(row, 8)
    copies = []
    for o, peer in enumerate(row_peers):
        copies.append(start(tiles.at[lax.rem(peer["row"], 8)], land2.at[row], s4.at[o], r4.at[o], peer))
    land2[row] = tiles[tile_no]

    z_core = [
        start(z.at[:, 2 * h + 1 - core], land_c.at[h], zs1.at[h], zr1.at[h], sibling) for h in range(2)
    ]

    for o in range(N_ROW - 1):
        copies[o].wait_recv()
    total = land2[0]
    for i in range(1, N_ROW):
        total = total + land2[i]
    spot = (
        pl.ds(pl.multiple_of(strip + 8 * (tile_no // 4), 8), 8),
        pl.ds(pl.multiple_of(128 * lax.rem(tile_no, 4), 128), 128),
    )
    out[spot] = total
    copies = []
    for i, o in enumerate((1, 2, 3, -1, -2, -3, -4)):
        peer = {"row": lax.rem(row + N_ROW + o, N_ROW)}
        copies.append(start(out.at[spot], out.at[spot], s5.at[i], r5.at[i], peer))

    for copy in z_core:
        copy.wait_recv()

    def add_core(i, carry):
        for h in range(2):
            land_c[h, i] = land_c[h, i] + z[i, 2 * h + core]
        return carry

    lax.fori_loop(0, N_ROW, add_core, 0)

    for copy in copies:
        copy.wait_recv()
    here = out.at[pl.ds(strip, 16)]
    copies = [start(here, here, s6.at[i], r6.at[i], peer) for i, peer in enumerate(plane)]
    onward = [start(here, here, s7.at[15], r7.at[15], sibling)]
    z_across = start(land_c.at[1 - half], land_x, zs2, zr2, across)
    for h in range(2):
        for o in range(N_COL):
            if h or o:
                i = h * N_COL + o - 1
                first = lax.rem(col + N_COL - o, N_COL) * 64 + (lax.rem(half + h, 2) * 2 + core) * 16
                there = out.at[pl.ds(pl.multiple_of(first, 16), 16)]
                copies[i].wait_recv()
                onward.append(start(there, there, s7.at[i], r7.at[i], sibling))

    z_across.wait_recv()

    def add_across(i, carry):
        land_x[i] = land_x[i] + land_c[half, i]
        return carry

    lax.fori_loop(0, N_ROW, add_across, 0)
    z_row = [
        start(land_x.at[peer["row"]], land_z.at[o], zs3.at[o], zr3.at[o], peer) for o, peer in enumerate(row_peers)
    ]
    for copy in onward:
        copy.wait_recv()

    n = gram.shape[0]
    eye = lax.broadcasted_iota(jnp.int32, (n, n), 0) == lax.broadcasted_iota(jnp.int32, (n, n), 1)
    whole = out[...]
    shift = 0.01 * jnp.sum(jnp.where(eye, whole, 0.0)) / n
    a_ref[...] = jnp.where(eye, whole + shift, whole)
    m_ref[...] = jnp.where(eye, 1.0, 0.0).astype(F32)
    z_rep = []
    for k in range(n // SPAN):
        end = (k + 1) * SPAN
        own, rest = slice(k * SPAN, end), slice(end, n)
        if end == n:
            z_sum = land_x[row]
            for o in range(N_ROW - 1):
                z_row[o].wait_recv()
                z_sum = z_sum + land_z[o]
            z_all[rep] = z_sum
            for o, peer in enumerate(rep_peers):
                z_rep.append(start(z_all.at[rep], z_all.at[rep], zs4.at[o], zr4.at[o], peer))
        inverse = invert_diagonal(a_ref[own, own])
        block = exact(inverse, m_ref[own, :end], ((1,), (0,)))
        m_ref[own, :end] = block
        if end < n:
            panel = exact(a_ref[rest, own], inverse, ((1,), (1,)))
            a_ref[rest, rest] = a_ref[rest, rest] - exact(panel, panel, ((1,), (1,)))
            m_ref[rest, :end] = m_ref[rest, :end] - exact(panel, block, ((1,), (0,)))

    for copy in z_rep:
        copy.wait_recv()
    new = exact(z_all[...].reshape(N_REP * 16, n), m_ref[...], ((1,), (1,)))
    lane = lax.broadcasted_iota(jnp.int32, (16, 128), 1) // 32
    for zz in range(N_ROW):
        base = 128 * (zz // 4)
        tile_out = jnp.zeros((16, 128), F32)
        for q in range(N_REP):
            block = new[16 * q : 16 * q + 16, base : base + 128]
            turn = (32 * (q - zz % 4)) % 128
            if turn:
                block = pltpu.roll(block, turn, 1)
            tile_out = jnp.where(lane == q, block, tile_out)
        packed[zz] = tile_out.astype(BF16)
    fac_ref[row] = packed[row]
    last = [
        start(packed.at[peer["row"]], fac_ref.at[row], fs.at[o], fr.at[o], peer) for o, peer in enumerate(row_peers)
    ]
    basis_ref[...] = exact(sk[...].astype(F32), m_ref[...], ((1,), (1,)))
    for copy in last:
        copy.wait_recv()
    for copy in sends:
        copy.wait_send()


def find_range(part, second):
    dma = pltpu.SemaphoreType.DMA
    vmem = pl.BlockSpec(memory_space=pltpu.VMEM)
    rows, rank = part.shape
    counts = (7, 7, 3, 15, 7, 15, 16)
    sems = []
    for count in counts:
        sems += [dma((count,))] * 2
    sems += [dma((2,)), dma((2,)), dma, dma, dma((15,)), dma((15,)), dma((3,)), dma((3,)), dma((15,)), dma((15,))]
    return pl.pallas_call(
        range_kernel,
        out_shape=(
            jax.ShapeDtypeStruct((rows, rank), F32),
            jax.ShapeDtypeStruct((N_ROW, 16, 128), BF16),
        ),
        in_specs=[vmem] * 2,
        out_specs=(vmem,) * 2,
        scratch_shapes=[
            pltpu.VMEM((rows, rank), BF16),
            pltpu.VMEM((N_COL - 1, rows // N_COL, rank), BF16),
            pltpu.VMEM((rows, rank), BF16),
            pltpu.VMEM((rank, rank), F32),
            pltpu.VMEM((rank, rank), F32),
            pltpu.VMEM((3, 16, rank), F32),
            pltpu.VMEM((8, 8, 128), F32),
            pltpu.VMEM((N_ROW, 8, 128), F32),
            pltpu.VMEM((N_ROW, N_REP, 16, rank), F32),
            pltpu.VMEM((2, N_ROW, 16, rank), F32),
            pltpu.VMEM((N_ROW, 16, rank), F32),
            pltpu.VMEM((N_ROW - 1, 16, rank), F32),
            pltpu.VMEM((N_REP, 16, rank), F32),
            pltpu.VMEM((N_ROW, 16, 128), BF16),
            pltpu.VMEM((rank, rank), F32),
            pltpu.VMEM((rank, rank), F32),
        ]
        + sems,
        compiler_params=pltpu.CompilerParams(collective_id=1, has_side_effects=True, vmem_limit_bytes=40 << 20),
        name="find_range",
    )(part, second)


def shards(tokens, out_grad, moment_old, basis_old, factor_old, test_matrix):
    tk, g, f = gather(tokens[0], out_grad[0], factor_old.T.astype(BF16))
    moment, second, part = tile(tk, g, f, moment_old, basis_old, test_matrix)
    basis_new, blocks = find_range(part, second)
    rank = factor_old.shape[1]
    factor_new = blocks.reshape(N_ROW, 16, N_REP, rank).transpose(0, 2, 1, 3).reshape(-1, rank).astype(F32)
    return (moment, basis_new, factor_new)


def solution(mesh):
    placed = (
        P("rep", "col", "row"),
        P("rep", "row", "col"),
        P(("row", "rep"), "col"),
        P(("row", "rep"), None),
        P("col", "row"),
        P("col", None),
    )
    return jax.shard_map(
        shards,
        mesh=mesh,
        in_specs=placed,
        out_specs=(P(("row", "rep"), "col"), P(("row", "rep"), None), P("col", "row")),
        check_vma=False,
    )
```

```python
import functools

import jax
import jax.numpy as jnp
from jax import lax
from jax.experimental import pallas as pl
from jax.experimental.pallas import tpu as pltpu
from jax.sharding import PartitionSpec as P

MESH = pl.DeviceIdType.MESH
F32 = jnp.float32
BF16 = jnp.bfloat16
N_ROW, N_COL, N_REP = 16, 8, 4


def remote(src, dst, send, recv, device):
    return pltpu.make_async_remote_copy(
        src_ref=src, dst_ref=dst, send_sem=send, recv_sem=recv, device_id=device, device_id_type=MESH
    )


def greet(devices):
    barrier = pltpu.get_barrier_semaphore()
    for device in devices:
        pl.semaphore_signal(barrier, inc=1, device_id=device, device_id_type=MESH)
    pl.semaphore_wait(barrier, len(devices))


def others(axis, size):
    me = lax.axis_index(axis)
    return [{axis: lax.rem(me + o, size)} for o in range(1, size)]


def gather_kernel(tok_ref, og_ref, fa_ref, tk_ref, g_ref, f_ref, rs, rr, ss, sr, xs, xr, ts, tr, cs, cr):
    row, col, rep = lax.axis_index("row"), lax.axis_index("col"), lax.axis_index("rep")
    half, core = rep // 2, lax.rem(rep, 2)
    across = (1 - half) * 2 + core
    sibling = half * 2 + 1 - core
    rep_peers = others("rep", N_REP)
    col_peers = others("col", N_COL)
    sides = ({"row": lax.rem(row + 1, N_ROW)}, {"row": lax.rem(row + N_ROW - 1, N_ROW)})
    wide = tok_ref.shape[1] // N_REP
    part = pl.ds(pl.multiple_of(rep * wide, wide), wide)
    g_ref[rep, row] = og_ref[...]
    f_ref[row, 0] = fa_ref[:16]
    f_ref[row, 1] = fa_ref[16:]
    tk_ref[col, rep] = tok_ref[:, part]
    greet(rep_peers + col_peers + list(sides))

    def slot(stream, z, c=core):
        if stream == 2:
            return f_ref.at[z, c]
        return g_ref.at[(half if stream == 0 else 1 - half) * 2 + c, z]

    def ring(stream, side, step):
        z = lax.rem(row + N_ROW + (1 - step if side == 0 else step - 1), N_ROW)
        return remote(slot(stream, z), slot(stream, z), rs.at[stream, side, step], rr.at[stream, side, step], sides[side])

    def arrival(stream, side, step):
        z = lax.rem(row + N_ROW + (-step if side == 0 else step), N_ROW)
        return remote(slot(stream, z), slot(stream, z), rs.at[stream, side, step], rr.at[stream, side, step], sides[side])

    def hand(stream, index, c=core):
        z = lax.rem(row + N_ROW + jnp.where(index <= 8, -index, index - 8), N_ROW)
        return remote(slot(stream, z, c), slot(stream, z, c), ss.at[stream, index], sr.at[stream, index], {"rep": sibling})

    swap = remote(slot(0, row), slot(0, row), xs, xr, {"rep": across})
    swap.start()
    for stream in (0, 2):
        for side in range(2):
            ring(stream, side, 1).start()
    first = []
    for o, peer in enumerate(rep_peers):
        start = pl.multiple_of(peer["rep"] * wide, wide)
        copy = remote(tok_ref.at[:, pl.ds(start, wide)], tk_ref.at[col, rep], ts.at[o], tr.at[o], peer)
        copy.start()
        first.append(copy)
    hand(0, 0).start()
    swap.wait_recv()
    for side in range(2):
        ring(1, side, 1).start()
    hand(1, 0).start()
    for copy in first:
        copy.wait_recv()
    second = []
    for o, peer in enumerate(col_peers):
        copy = remote(tk_ref.at[col], tk_ref.at[col], cs.at[o], cr.at[o], peer)
        copy.start()
        second.append(copy)

    def step(s, carry):
        for stream in (0, 2, 1):
            arrival(stream, 0, s).wait_recv()
            ring(stream, 0, s + 1).start()
            hand(stream, s).start()
            arrival(stream, 1, s).wait_recv()

            @pl.when(s < 7)
            def _():
                ring(stream, 1, s + 1).start()

            hand(stream, s + 8).start()
        return carry

    lax.fori_loop(1, 8, step, 0)
    for stream in (0, 2, 1):
        arrival(stream, 0, 8).wait_recv()
        hand(stream, 8).start()
    for copy in second:
        copy.wait_recv()

    def finish(i, carry):
        for stream in range(3):
            hand(stream, i, 1 - core).wait_recv()
            hand(stream, i).wait_send()
        return carry

    for stream in range(2):
        hand(stream, 0, 1 - core).wait_recv()
        hand(stream, 0).wait_send()
    lax.fori_loop(1, 16, finish, 0)

    def drain(s, carry):
        for stream in range(3):
            for side in range(2):
                ring(stream, side, s).wait_send()
        return carry

    lax.fori_loop(1, 8, drain, 0)
    for stream in range(3):
        ring(stream, 0, 8).wait_send()
    swap.wait_send()
    for copy in first + second:
        copy.wait_send()


def gather(tokens, out_grad, factor):
    dma = pltpu.SemaphoreType.DMA
    vmem = pl.BlockSpec(memory_space=pltpu.VMEM)
    depth, wide = tokens.shape[0], tokens.shape[1] // N_REP
    tall, across = out_grad.shape
    return pl.pallas_call(
        gather_kernel,
        out_shape=(
            jax.ShapeDtypeStruct((N_COL, N_REP, depth, wide), BF16),
            jax.ShapeDtypeStruct((N_REP, N_ROW, tall, across), BF16),
            jax.ShapeDtypeStruct((N_ROW, 2, factor.shape[0] // 2, across), BF16),
        ),
        in_specs=[vmem] * 3,
        out_specs=(vmem,) * 3,
        scratch_shapes=[
            dma((3, 2, 9)), dma((3, 2, 9)), dma((3, 16)), dma((3, 16)), dma, dma,
            dma((3,)), dma((3,)), dma((7,)), dma((7,)),
        ],
        compiler_params=pltpu.CompilerParams(collective_id=4, has_side_effects=True, vmem_limit_bytes=12 << 20),
        name="gather",
    )(tokens, out_grad, factor)


def tile_kernel(tk_ref, g_ref, f_ref, moment_ref, basis_ref, test_ref, new_ref, second_ref, part_ref, high, low):
    step = 256
    high[...] = basis_ref[...].astype(BF16)
    low[...] = (basis_ref[...] - high[...].astype(F32)).astype(BF16)
    rank = basis_ref.shape[1]
    part_ref[...] = jnp.zeros_like(part_ref)

    def columns(i, carry):
        here = pl.ds(pl.multiple_of(i * step, step), step)
        gradient = jnp.zeros((new_ref.shape[0], step), F32)
        for b in range(N_REP):
            left = tk_ref[:, b].reshape(-1, tk_ref.shape[3])
            right = g_ref[b, :, :, here].reshape(-1, step)
            piece = lax.dot_general(left, right, (((0,), (0,)), ((), ())), preferred_element_type=F32)
            gradient = gradient + piece.astype(BF16).astype(F32)
        new_ref[:, here] = 0.9 * moment_ref[:, here] + 0.1 * gradient
        factor = f_ref[:, :, :, here].reshape(rank, step)
        previous = jnp.dot(high[...], factor, preferred_element_type=F32)
        previous = previous + jnp.dot(low[...], factor, preferred_element_type=F32)
        second = (0.95 * previous + 0.05 * gradient * gradient).astype(BF16)
        second_ref[:, here] = second
        part_ref[...] += jnp.dot(second, test_ref[here], preferred_element_type=F32)
        return carry

    lax.fori_loop(0, new_ref.shape[1] // step, columns, 0)


def tile(tk, g, f, moment_old, basis_old, test_matrix):
    vmem = pl.BlockSpec(memory_space=pltpu.VMEM)
    rows, columns = moment_old.shape
    rank = basis_old.shape[1]
    return pl.pallas_call(
        tile_kernel,
        out_shape=(
            jax.ShapeDtypeStruct((rows, columns), F32),
            jax.ShapeDtypeStruct((rows, columns), BF16),
            jax.ShapeDtypeStruct((rows, rank), F32),
        ),
        in_specs=[vmem] * 6,
        out_specs=(vmem,) * 3,
        scratch_shapes=[pltpu.VMEM((rows, rank), BF16)] * 2,
        compiler_params=pltpu.CompilerParams(vmem_limit_bytes=20 << 20),
        name="tile",
    )(tk, g, f, moment_old, basis_old, test_matrix)


SPAN = 128


def invert_diagonal(block):
    sub = lax.broadcasted_iota(jnp.int32, (8, SPAN), 0)
    shape = (SPAN, SPAN)
    d = block
    x = (lax.broadcasted_iota(jnp.int32, shape, 0) == lax.broadcasted_iota(jnp.int32, shape, 1)).astype(F32)
    out = []

    def spread(value):
        return jnp.broadcast_to(value, (8, SPAN))

    for j0 in range(0, SPAN, 8):
        wide = [spread(d[:8, j0 + m : j0 + m + 1]) for m in range(8)]
        s = [[spread(wide[m][i : i + 1, :]) if m <= i else None for m in range(8)] for i in range(8)]
        p = [spread(d[i : i + 1, :]) for i in range(8)]
        q = [spread(x[i : i + 1, :]) for i in range(8)]
        inverse = [None] * 8
        f = [[None] * 8 for _ in range(8)]
        for m in range(8):
            inverse[m] = 1.0 / s[m][m]
            for i in range(m + 1, 8):
                f[i][m] = s[i][m] * inverse[m]
            for i in range(m + 1, 8):
                for l in range(m + 1, i + 1):
                    s[i][l] = s[i][l] - f[i][m] * s[l][m]
            for i in range(m + 1, 8):
                p[i] = p[i] - f[i][m] * p[m]
                q[i] = q[i] - f[i][m] * q[m]
        done = q[0] * lax.rsqrt(s[0][0])
        for i in range(1, 8):
            done = jnp.where(sub == i, q[i] * lax.rsqrt(s[i][i]), done)
        out.append(done)
        if j0 + 8 == SPAN:
            break
        v, w = [None] * 8, [None] * 8
        for i in reversed(range(8)):
            v[i] = p[i] * inverse[i]
            w[i] = q[i] * inverse[i]
            for m in range(i + 1, 8):
                v[i] = v[i] - f[m][i] * v[m]
                w[i] = w[i] - f[m][i] * w[m]
        d, x = d[8:], x[8:]
        source = d
        for m in range(8):
            c = source[:, j0 + m : j0 + m + 1]
            d = d - c * v[m][:1]
            x = x - c * w[m][:1]
    return jnp.concatenate(out, 0)


def exact(a, b, dims):
    return lax.dot_general(a, b, (dims, ((), ())), precision=lax.Precision.HIGHEST, preferred_element_type=F32)


def range_kernel(
    part_ref, second_ref, basis_ref, fac_ref,
    send_sk, land_sk, sk, gram, out, land1, tiles, land2, z, land_c, land_x, land_z, z_all, packed, m_ref, a_ref, away_x, z_half,
    s1, r1, s2, r2, s3, r3, s4, r4, s5, r5, s6, r6, s7, r7, zs1, zr1, zs2, zr2, zs3, zr3, zs4, zr4, fs, fr,
):
    row, col, rep = lax.axis_index("row"), lax.axis_index("col"), lax.axis_index("rep")
    half, core = rep // 2, lax.rem(rep, 2)
    rep_peers = others("rep", N_REP)
    row_peers = others("row", N_ROW)
    col_peers = others("col", N_COL)
    sibling = {"rep": half * 2 + 1 - core}
    across = {"rep": (1 - half) * 2 + core}
    plane = []
    for h in range(2):
        for o in range(N_COL):
            if h or o:
                plane.append({"col": lax.rem(col + o, N_COL), "rep": lax.rem(half + h, 2) * 2 + core})
    sends = []

    def start(src, dst, send, recv, device):
        copy = remote(src, dst, send, recv, device)
        copy.start()
        sends.append(copy)
        return copy

    send_sk[...] = part_ref[...].astype(BF16)
    greet(rep_peers + row_peers + plane)
    rows = part_ref.shape[0] // N_COL
    mine = pl.ds(pl.multiple_of(col * rows, rows), rows)
    copies = []
    for o, peer in enumerate(col_peers):
        there = pl.ds(pl.multiple_of(peer["col"] * rows, rows), rows)
        copies.append(start(send_sk.at[there], land_sk.at[o], s1.at[o], r1.at[o], peer))
    total = part_ref[mine]
    for o in range(N_COL - 1):
        copies[o].wait_recv()
        total = total + land_sk[o].astype(F32)
    sk[mine] = total.astype(BF16)
    copies = [start(sk.at[mine], sk.at[mine], s2.at[o], r2.at[o], peer) for o, peer in enumerate(col_peers)]
    for copy in copies:
        copy.wait_recv()

    sketch = sk[...]
    gram[...] = lax.dot_general(sketch, sketch, (((0,), (0,)), ((), ())), preferred_element_type=F32)
    copies = []
    for o, peer in enumerate(rep_peers):
        there = pl.ds(pl.multiple_of(col * 64 + peer["rep"] * 16, 16), 16)
        copies.append(start(gram.at[there], land1.at[o], s3.at[o], r3.at[o], peer))

    for i in range(4):
        piece = lax.dot_general(
            second_ref[:, 256 * i : 256 * i + 256], sketch, (((0,), (0,)), ((), ())), preferred_element_type=F32
        )
        z[4 * i : 4 * i + 4] = piece.reshape(4, N_REP, 16, sketch.shape[1])

    strip = pl.multiple_of(col * 64 + rep * 16, 16)
    total = gram[pl.ds(strip, 16)]
    for o in range(N_REP - 1):
        copies[o].wait_recv()
        total = total + land1[o]
    for t in range(8):
        tiles[t] = total[8 * (t // 4) : 8 * (t // 4) + 8, 128 * (t % 4) : 128 * (t % 4) + 128]
    tile_no = lax.rem(row, 8)
    copies = []
    for o, peer in enumerate(row_peers):
        copies.append(start(tiles.at[lax.rem(peer["row"], 8)], land2.at[row], s4.at[o], r4.at[o], peer))
    land2[row] = tiles[tile_no]

    z_core = [
        start(z.at[:, 2 * h + 1 - core], land_c.at[h], zs1.at[h], zr1.at[h], sibling) for h in range(2)
    ]

    for copy in z_core:
        copy.wait_recv()

    def add_core(i, carry):
        away_x[i] = (land_c[1 - half, i] + z[i, 2 * (1 - half) + core]).astype(BF16)
        return carry

    lax.fori_loop(0, N_ROW, add_core, 0)
    z_across = start(away_x, land_x, zs2, zr2, across)

    for o in range(N_ROW - 1):
        copies[o].wait_recv()
    total = land2[0]
    for i in range(1, N_ROW):
        total = total + land2[i]
    spot = (
        pl.ds(pl.multiple_of(strip + 8 * (tile_no // 4), 8), 8),
        pl.ds(pl.multiple_of(128 * lax.rem(tile_no, 4), 128), 128),
    )
    out[spot] = total
    copies = []
    for i, o in enumerate((1, 2, 3, -1, -2, -3, -4)):
        peer = {"row": lax.rem(row + N_ROW + o, N_ROW)}
        copies.append(start(out.at[spot], out.at[spot], s5.at[i], r5.at[i], peer))

    for copy in copies:
        copy.wait_recv()
    here = out.at[pl.ds(strip, 16)]
    copies = [start(here, here, s6.at[i], r6.at[i], peer) for i, peer in enumerate(plane)]
    onward = [start(here, here, s7.at[15], r7.at[15], sibling)]
    z_row = []

    def add_across(i, carry):
        z_half[i] = (land_x[i].astype(F32) + land_c[half, i]) + z[i, 2 * half + core]
        return carry

    for h in range(2):
        if h == 1:
            z_across.wait_recv()
            lax.fori_loop(0, N_ROW, add_across, 0)
            for o, peer in enumerate(row_peers):
                z_row.append(start(z_half.at[peer["row"]], land_z.at[o], zs3.at[o], zr3.at[o], peer))
        for o in range(N_COL):
            if h or o:
                i = h * N_COL + o - 1
                first = lax.rem(col + N_COL - o, N_COL) * 64 + (lax.rem(half + h, 2) * 2 + core) * 16
                there = out.at[pl.ds(pl.multiple_of(first, 16), 16)]
                copies[i].wait_recv()
                onward.append(start(there, there, s7.at[i], r7.at[i], sibling))

    for copy in onward:
        copy.wait_recv()

    n = gram.shape[0]
    eye = lax.broadcasted_iota(jnp.int32, (n, n), 0) == lax.broadcasted_iota(jnp.int32, (n, n), 1)
    whole = out[...]
    shift = 0.01 * jnp.sum(jnp.where(eye, whole, 0.0)) / n
    a_ref[...] = jnp.where(eye, whole + shift, whole)
    m_ref[...] = jnp.where(eye, 1.0, 0.0).astype(F32)
    z_rep = []
    for k in range(n // SPAN):
        end = (k + 1) * SPAN
        own, rest = slice(k * SPAN, end), slice(end, n)
        if end == n:
            z_sum = z_half[row]
            for o in range(N_ROW - 1):
                z_row[o].wait_recv()
                z_sum = z_sum + land_z[o]
            z_all[rep] = z_sum
            for o, peer in enumerate(rep_peers):
                z_rep.append(start(z_all.at[rep], z_all.at[rep], zs4.at[o], zr4.at[o], peer))
        inverse = invert_diagonal(a_ref[own, own])
        block = exact(inverse, m_ref[own, :end], ((1,), (0,)))
        m_ref[own, :end] = block
        if end < n:
            panel = exact(a_ref[rest, own], inverse, ((1,), (1,)))
            a_ref[rest, rest] = a_ref[rest, rest] - exact(panel, panel, ((1,), (1,)))
            m_ref[rest, :end] = m_ref[rest, :end] - exact(panel, block, ((1,), (0,)))

    for copy in z_rep:
        copy.wait_recv()
    new = exact(z_all[...].reshape(N_REP * 16, n), m_ref[...], ((1,), (1,)))
    lane = lax.broadcasted_iota(jnp.int32, (16, 128), 1) // 32
    for zz in range(N_ROW):
        base = 128 * (zz // 4)
        tile_out = jnp.zeros((16, 128), F32)
        for q in range(N_REP):
            block = new[16 * q : 16 * q + 16, base : base + 128]
            turn = (32 * (q - zz % 4)) % 128
            if turn:
                block = pltpu.roll(block, turn, 1)
            tile_out = jnp.where(lane == q, block, tile_out)
        packed[zz] = tile_out.astype(BF16)
    fac_ref[row] = packed[row]
    last = [
        start(packed.at[peer["row"]], fac_ref.at[row], fs.at[o], fr.at[o], peer) for o, peer in enumerate(row_peers)
    ]
    basis_ref[...] = exact(sk[...].astype(F32), m_ref[...], ((1,), (1,)))
    for copy in last:
        copy.wait_recv()
    for copy in sends:
        copy.wait_send()


def find_range(part, second):
    dma = pltpu.SemaphoreType.DMA
    vmem = pl.BlockSpec(memory_space=pltpu.VMEM)
    rows, rank = part.shape
    counts = (7, 7, 3, 15, 7, 15, 16)
    sems = []
    for count in counts:
        sems += [dma((count,))] * 2
    sems += [dma((2,)), dma((2,)), dma, dma, dma((15,)), dma((15,)), dma((3,)), dma((3,)), dma((15,)), dma((15,))]
    return pl.pallas_call(
        range_kernel,
        out_shape=(
            jax.ShapeDtypeStruct((rows, rank), F32),
            jax.ShapeDtypeStruct((N_ROW, 16, 128), BF16),
        ),
        in_specs=[vmem] * 2,
        out_specs=(vmem,) * 2,
        scratch_shapes=[
            pltpu.VMEM((rows, rank), BF16),
            pltpu.VMEM((N_COL - 1, rows // N_COL, rank), BF16),
            pltpu.VMEM((rows, rank), BF16),
            pltpu.VMEM((rank, rank), F32),
            pltpu.VMEM((rank, rank), F32),
            pltpu.VMEM((3, 16, rank), F32),
            pltpu.VMEM((8, 8, 128), F32),
            pltpu.VMEM((N_ROW, 8, 128), F32),
            pltpu.VMEM((N_ROW, N_REP, 16, rank), F32),
            pltpu.VMEM((2, N_ROW, 16, rank), F32),
            pltpu.VMEM((N_ROW, 16, rank), BF16),
            pltpu.VMEM((N_ROW - 1, 16, rank), F32),
            pltpu.VMEM((N_REP, 16, rank), F32),
            pltpu.VMEM((N_ROW, 16, 128), BF16),
            pltpu.VMEM((rank, rank), F32),
            pltpu.VMEM((rank, rank), F32),
            pltpu.VMEM((N_ROW, 16, rank), BF16),
            pltpu.VMEM((N_ROW, 16, rank), F32),
        ]
        + sems,
        compiler_params=pltpu.CompilerParams(collective_id=1, has_side_effects=True, vmem_limit_bytes=40 << 20),
        name="find_range",
    )(part, second)


def shards(tokens, out_grad, moment_old, basis_old, factor_old, test_matrix):
    tk, g, f = gather(tokens[0], out_grad[0], factor_old.T.astype(BF16))
    moment, second, part = tile(tk, g, f, moment_old, basis_old, test_matrix)
    basis_new, blocks = find_range(part, second)
    rank = factor_old.shape[1]
    factor_new = blocks.reshape(N_ROW, 16, N_REP, rank).transpose(0, 2, 1, 3).reshape(-1, rank).astype(F32)
    return (moment, basis_new, factor_new)


def solution(mesh):
    placed = (
        P("rep", "col", "row"),
        P("rep", "row", "col"),
        P(("row", "rep"), "col"),
        P(("row", "rep"), None),
        P("col", "row"),
        P("col", None),
    )
    return jax.shard_map(
        shards,
        mesh=mesh,
        in_specs=placed,
        out_specs=(P(("row", "rep"), "col"), P(("row", "rep"), None), P("col", "row")),
        check_vma=False,
    )
```

```python
import functools

import jax
import jax.numpy as jnp
from jax import lax
from jax.experimental import pallas as pl
from jax.experimental.pallas import tpu as pltpu
from jax.sharding import PartitionSpec as P

MESH = pl.DeviceIdType.MESH
F32 = jnp.float32
BF16 = jnp.bfloat16
N_ROW, N_COL, N_REP = 16, 8, 4


def remote(src, dst, send, recv, device):
    return pltpu.make_async_remote_copy(
        src_ref=src, dst_ref=dst, send_sem=send, recv_sem=recv, device_id=device, device_id_type=MESH
    )


def greet(devices):
    barrier = pltpu.get_barrier_semaphore()
    for device in devices:
        pl.semaphore_signal(barrier, inc=1, device_id=device, device_id_type=MESH)
    pl.semaphore_wait(barrier, len(devices))


def others(axis, size):
    me = lax.axis_index(axis)
    return [{axis: lax.rem(me + o, size)} for o in range(1, size)]


HOPS = (
    (0, 4), (0, 8), (0, 12), (0, 1), (0, -1), (0, 2),
    (4, 1), (4, -1), (4, 2), (4, -2),
    (8, 1), (8, -1), (8, -2),
    (12, 1), (12, -1),
)
NEAR = ((0, 1, 2), (3, 6, 10, 13), (4, 7, 11, 14), (5, 8, 9, 12))


def tile_kernel(
    tok_ref, og_ref, fa_ref, moment_ref, basis_ref, test_ref, new_ref, second_ref, part_ref,
    tk, g, f, old_f, old_m, old_b, test, high, low, zs, zr, xs, xr, ss, sr, ts, tr, cs, cr, local,
):
    row, col, rep = lax.axis_index("row"), lax.axis_index("col"), lax.axis_index("rep")
    half, core = rep // 2, lax.rem(rep, 2)
    across = (1 - half) * 2 + core
    sibling = half * 2 + 1 - core
    corner = (1 - half) * 2 + 1 - core
    rep_peers = others("rep", N_REP)
    col_peers = others("col", N_COL)

    def at(offset):
        return lax.rem(row + N_ROW + offset, N_ROW)

    wide = tok_ref.shape[1] // N_REP
    part = pl.ds(pl.multiple_of(rep * wide, wide), wide)
    own = [
        pltpu.make_async_copy(og_ref, g.at[rep, row // 4, lax.rem(row, 4)], local.at[0]),
        pltpu.make_async_copy(fa_ref, old_f, local.at[1]),
        pltpu.make_async_copy(tok_ref.at[:, part], tk.at[col, rep], local.at[2]),
        pltpu.make_async_copy(moment_ref, old_m, local.at[3]),
        pltpu.make_async_copy(basis_ref, old_b, local.at[4]),
        pltpu.make_async_copy(test_ref, test, local.at[5]),
    ]
    for copy in own:
        copy.start()
    greet(rep_peers + col_peers + [{"row": at(o)} for o in (1, -1, 2, -2, 4, 8, 12)])

    def slot(stream, z):
        if stream:
            return f.at[z // 4, lax.rem(z, 4), core]
        return g.at[rep, z // 4, lax.rem(z, 4)]

    def hop(stream, i, arriving=False):
        d, o = HOPS[i]
        here = slot(stream, at(d - o if arriving else d))
        return remote(here, here, zs.at[stream, i], zr.at[stream, i], {"row": at(o)})

    classes = [lax.rem(row + 4 + o, 4) for o in (0, -1, 1, 2)]

    def over(j, arriving=False):
        here = g.at[across if arriving else rep, :, classes[j]]
        return remote(here, here, xs.at[j], xr.at[j], {"rep": across})

    def hand(kind, j, arriving=False):
        if kind == 2:
            here = f.at[:, classes[j], (1 - core) if arriving else core]
        elif kind == 1:
            here = g.at[corner if arriving else across, :, classes[j]]
        else:
            here = g.at[sibling if arriving else rep, :, classes[j]]
        return remote(here, here, ss.at[kind, j], sr.at[kind, j], {"rep": sibling})

    sends = []

    def go(copy):
        copy.start()
        sends.append(copy)

    own[0].wait()
    for i in range(6):
        go(hop(0, i))
    first = []
    for o, peer in enumerate(rep_peers):
        there = pl.ds(pl.multiple_of(peer["rep"] * wide, wide), wide)
        copy = remote(tok_ref.at[:, there], tk.at[col, rep], ts.at[o], tr.at[o], peer)
        go(copy)
        first.append(copy)
    own[1].wait()
    f[row // 4, lax.rem(row, 4), core] = old_f[pl.ds(pl.multiple_of(16 * core, 16), 16)].astype(BF16)
    for i in range(6):
        go(hop(1, i))
    for stream in range(2):
        for i, onward in ((0, (13, 14)), (2, (6, 7, 8, 9)), (1, (10, 11, 12))):
            hop(stream, i, True).wait_recv()
            for k in onward:
                go(hop(stream, k))
        if stream == 0:
            go(over(0))
            go(hand(0, 0))
            own[2].wait()
            for copy in first:
                copy.wait_recv()
            second = []
            for o, peer in enumerate(col_peers):
                copy = remote(tk.at[col], tk.at[col], cs.at[o], cr.at[o], peer)
                go(copy)
                second.append(copy)
        else:
            go(hand(2, 0))
    for j in (1, 2, 3):
        for i in NEAR[j]:
            hop(0, i, True).wait_recv()
        go(over(j))
        go(hand(0, j))
    for j in (0, 1):
        over(j, True).wait_recv()
        go(hand(1, j))
    for j in (1, 2, 3):
        for i in NEAR[j]:
            hop(1, i, True).wait_recv()
        go(hand(2, j))
    for j in (2, 3):
        over(j, True).wait_recv()
        go(hand(1, j))
    for copy in own[3:]:
        copy.wait()
    high[...] = old_b[...].astype(BF16)
    low[...] = (old_b[...] - high[...].astype(F32)).astype(BF16)
    part_ref[...] = jnp.zeros_like(part_ref)
    for copy in second:
        copy.wait_recv()
    for j in range(4):
        for kind in range(3):
            hand(kind, j, True).wait_recv()

    step = 256
    rank = old_b.shape[1]

    def columns(i, carry):
        here = pl.ds(pl.multiple_of(i * step, step), step)
        gradient = jnp.zeros((new_ref.shape[0], step), F32)
        for b in range(N_REP):
            left = tk[:, b].reshape(-1, wide)
            right = g[b, :, :, :, here].reshape(-1, step)
            piece = lax.dot_general(left, right, (((0,), (0,)), ((), ())), preferred_element_type=F32)
            gradient = gradient + piece.astype(BF16).astype(F32)
        new_ref[:, here] = 0.9 * old_m[:, here] + 0.1 * gradient
        factor = f[:, :, :, :, here].reshape(rank, step)
        previous = jnp.dot(high[...], factor, preferred_element_type=F32)
        previous = previous + jnp.dot(low[...], factor, preferred_element_type=F32)
        second_tile = (0.95 * previous + 0.05 * gradient * gradient).astype(BF16)
        second_ref[:, here] = second_tile
        part_ref[...] += jnp.dot(second_tile, test[here], preferred_element_type=F32)
        return carry

    lax.fori_loop(0, new_ref.shape[1] // step, columns, 0)
    for copy in sends:
        copy.wait_send()


def tile(tokens, out_grad, factor, moment_old, basis_old, test_matrix):
    dma = pltpu.SemaphoreType.DMA
    vmem = pl.BlockSpec(memory_space=pltpu.VMEM)
    hbm = pl.BlockSpec(memory_space=pltpu.HBM)
    depth, wide = tokens.shape[0], tokens.shape[1] // N_REP
    tall = out_grad.shape[0]
    rows, columns = moment_old.shape
    rank = basis_old.shape[1]
    return pl.pallas_call(
        tile_kernel,
        out_shape=(
            jax.ShapeDtypeStruct((rows, columns), F32),
            jax.ShapeDtypeStruct((rows, columns), BF16),
            jax.ShapeDtypeStruct((rows, rank), F32),
        ),
        in_specs=[hbm] * 6,
        out_specs=(vmem,) * 3,
        scratch_shapes=[
            pltpu.VMEM((N_COL, N_REP, depth, wide), BF16),
            pltpu.VMEM((N_REP, 4, 4, tall, columns), BF16),
            pltpu.VMEM((4, 4, 2, factor.shape[0] // 2, columns), BF16),
            pltpu.VMEM(factor.shape, F32),
            pltpu.VMEM(moment_old.shape, F32),
            pltpu.VMEM(basis_old.shape, F32),
            pltpu.VMEM(test_matrix.shape, BF16),
            pltpu.VMEM((rows, rank), BF16),
            pltpu.VMEM((rows, rank), BF16),
            dma((2, 15)), dma((2, 15)), dma((4,)), dma((4,)), dma((3, 4)), dma((3, 4)),
            dma((3,)), dma((3,)), dma((7,)), dma((7,)), dma((6,)),
        ],
        compiler_params=pltpu.CompilerParams(
            collective_id=4, has_side_effects=True, vmem_limit_bytes=54 << 20
        ),
        name="tile",
    )(tokens, out_grad, factor, moment_old, basis_old, test_matrix)


SPAN = 128


def invert_diagonal(block):
    sub = lax.broadcasted_iota(jnp.int32, (8, SPAN), 0)
    shape = (SPAN, SPAN)
    d = block
    x = (lax.broadcasted_iota(jnp.int32, shape, 0) == lax.broadcasted_iota(jnp.int32, shape, 1)).astype(F32)
    out = []

    def spread(value):
        return jnp.broadcast_to(value, (8, SPAN))

    for j0 in range(0, SPAN, 8):
        wide = [spread(d[:8, j0 + m : j0 + m + 1]) for m in range(8)]
        s = [[spread(wide[m][i : i + 1, :]) if m <= i else None for m in range(8)] for i in range(8)]
        p = [spread(d[i : i + 1, :]) for i in range(8)]
        q = [spread(x[i : i + 1, :]) for i in range(8)]
        inverse = [None] * 8
        f = [[None] * 8 for _ in range(8)]
        for m in range(8):
            inverse[m] = 1.0 / s[m][m]
            for i in range(m + 1, 8):
                f[i][m] = s[i][m] * inverse[m]
            for i in range(m + 1, 8):
                for l in range(m + 1, i + 1):
                    s[i][l] = s[i][l] - f[i][m] * s[l][m]
            for i in range(m + 1, 8):
                p[i] = p[i] - f[i][m] * p[m]
                q[i] = q[i] - f[i][m] * q[m]
        done = q[0] * lax.rsqrt(s[0][0])
        for i in range(1, 8):
            done = jnp.where(sub == i, q[i] * lax.rsqrt(s[i][i]), done)
        out.append(done)
        if j0 + 8 == SPAN:
            break
        v, w = [None] * 8, [None] * 8
        for i in reversed(range(8)):
            v[i] = p[i] * inverse[i]
            w[i] = q[i] * inverse[i]
            for m in range(i + 1, 8):
                v[i] = v[i] - f[m][i] * v[m]
                w[i] = w[i] - f[m][i] * w[m]
        d, x = d[8:], x[8:]
        source = d
        for m in range(8):
            c = source[:, j0 + m : j0 + m + 1]
            d = d - c * v[m][:1]
            x = x - c * w[m][:1]
    return jnp.concatenate(out, 0)


def exact(a, b, dims):
    return lax.dot_general(a, b, (dims, ((), ())), precision=lax.Precision.HIGHEST, preferred_element_type=F32)


def range_kernel(
    part_ref, second_ref, basis_ref, fac_ref,
    send_sk, land_sk, sk, gram, out, land1, tiles, land2, z, land_c, land_x, land_z, z_all, packed, m_ref, a_ref, away_x, z_half,
    s1, r1, s2, r2, s3, r3, s4, r4, s5, r5, s6, r6, s7, r7, zs1, zr1, zs2, zr2, zs3, zr3, zs4, zr4, fs, fr,
):
    row, col, rep = lax.axis_index("row"), lax.axis_index("col"), lax.axis_index("rep")
    half, core = rep // 2, lax.rem(rep, 2)
    rep_peers = others("rep", N_REP)
    row_peers = others("row", N_ROW)
    col_peers = others("col", N_COL)
    sibling = {"rep": half * 2 + 1 - core}
    across = {"rep": (1 - half) * 2 + core}
    plane = []
    for h in range(2):
        for o in range(N_COL):
            if h or o:
                plane.append({"col": lax.rem(col + o, N_COL), "rep": lax.rem(half + h, 2) * 2 + core})
    sends = []

    def start(src, dst, send, recv, device):
        copy = remote(src, dst, send, recv, device)
        copy.start()
        sends.append(copy)
        return copy

    send_sk[...] = part_ref[...].astype(BF16)
    greet(rep_peers + row_peers + plane)
    rows = part_ref.shape[0] // N_COL
    mine = pl.ds(pl.multiple_of(col * rows, rows), rows)
    copies = []
    for o, peer in enumerate(col_peers):
        there = pl.ds(pl.multiple_of(peer["col"] * rows, rows), rows)
        copies.append(start(send_sk.at[there], land_sk.at[o], s1.at[o], r1.at[o], peer))
    total = part_ref[mine]
    for o in range(N_COL - 1):
        copies[o].wait_recv()
        total = total + land_sk[o].astype(F32)
    sk[mine] = total.astype(BF16)
    copies = [start(sk.at[mine], sk.at[mine], s2.at[o], r2.at[o], peer) for o, peer in enumerate(col_peers)]
    for copy in copies:
        copy.wait_recv()

    sketch = sk[...]
    gram[...] = lax.dot_general(sketch, sketch, (((0,), (0,)), ((), ())), preferred_element_type=F32)
    copies = []
    for o, peer in enumerate(rep_peers):
        there = pl.ds(pl.multiple_of(col * 64 + peer["rep"] * 16, 16), 16)
        copies.append(start(gram.at[there], land1.at[o], s3.at[o], r3.at[o], peer))

    for i in range(4):
        piece = lax.dot_general(
            second_ref[:, 256 * i : 256 * i + 256], sketch, (((0,), (0,)), ((), ())), preferred_element_type=F32
        )
        z[4 * i : 4 * i + 4] = piece.reshape(4, N_REP, 16, sketch.shape[1])

    strip = pl.multiple_of(col * 64 + rep * 16, 16)
    total = gram[pl.ds(strip, 16)]
    for o in range(N_REP - 1):
        copies[o].wait_recv()
        total = total + land1[o]
    for t in range(8):
        tiles[t] = total[8 * (t // 4) : 8 * (t // 4) + 8, 128 * (t % 4) : 128 * (t % 4) + 128]
    tile_no = lax.rem(row, 8)
    copies = []
    for o, peer in enumerate(row_peers):
        copies.append(start(tiles.at[lax.rem(peer["row"], 8)], land2.at[row], s4.at[o], r4.at[o], peer))
    land2[row] = tiles[tile_no]

    z_core = [
        start(z.at[:, 2 * h + 1 - core], land_c.at[h], zs1.at[h], zr1.at[h], sibling) for h in range(2)
    ]

    for copy in z_core:
        copy.wait_recv()

    def add_core(i, carry):
        away_x[i] = (land_c[1 - half, i] + z[i, 2 * (1 - half) + core]).astype(BF16)
        return carry

    lax.fori_loop(0, N_ROW, add_core, 0)
    z_across = start(away_x, land_x, zs2, zr2, across)

    for o in range(N_ROW - 1):
        copies[o].wait_recv()
    total = land2[0]
    for i in range(1, N_ROW):
        total = total + land2[i]
    spot = (
        pl.ds(pl.multiple_of(strip + 8 * (tile_no // 4), 8), 8),
        pl.ds(pl.multiple_of(128 * lax.rem(tile_no, 4), 128), 128),
    )
    out[spot] = total
    copies = []
    for i, o in enumerate((1, 2, 3, -1, -2, -3, -4)):
        peer = {"row": lax.rem(row + N_ROW + o, N_ROW)}
        copies.append(start(out.at[spot], out.at[spot], s5.at[i], r5.at[i], peer))

    for copy in copies:
        copy.wait_recv()
    here = out.at[pl.ds(strip, 16)]
    copies = [start(here, here, s6.at[i], r6.at[i], peer) for i, peer in enumerate(plane)]
    onward = [start(here, here, s7.at[15], r7.at[15], sibling)]
    z_row = []

    def add_across(i, carry):
        z_half[i] = (land_x[i].astype(F32) + land_c[half, i]) + z[i, 2 * half + core]
        return carry

    for h in range(2):
        if h == 1:
            z_across.wait_recv()
            lax.fori_loop(0, N_ROW, add_across, 0)
            for o, peer in enumerate(row_peers):
                z_row.append(start(z_half.at[peer["row"]], land_z.at[o], zs3.at[o], zr3.at[o], peer))
        for o in range(N_COL):
            if h or o:
                i = h * N_COL + o - 1
                first = lax.rem(col + N_COL - o, N_COL) * 64 + (lax.rem(half + h, 2) * 2 + core) * 16
                there = out.at[pl.ds(pl.multiple_of(first, 16), 16)]
                copies[i].wait_recv()
                onward.append(start(there, there, s7.at[i], r7.at[i], sibling))

    for copy in onward:
        copy.wait_recv()

    n = gram.shape[0]
    eye = lax.broadcasted_iota(jnp.int32, (n, n), 0) == lax.broadcasted_iota(jnp.int32, (n, n), 1)
    whole = out[...]
    shift = 0.01 * jnp.sum(jnp.where(eye, whole, 0.0)) / n
    a_ref[...] = jnp.where(eye, whole + shift, whole)
    m_ref[...] = jnp.where(eye, 1.0, 0.0).astype(F32)
    z_rep = []
    for k in range(n // SPAN):
        end = (k + 1) * SPAN
        own, rest = slice(k * SPAN, end), slice(end, n)
        if end == n:
            z_sum = z_half[row]
            for o in range(N_ROW - 1):
                z_row[o].wait_recv()
                z_sum = z_sum + land_z[o]
            z_all[rep] = z_sum
            for o, peer in enumerate(rep_peers):
                z_rep.append(start(z_all.at[rep], z_all.at[rep], zs4.at[o], zr4.at[o], peer))
        inverse = invert_diagonal(a_ref[own, own])
        block = exact(inverse, m_ref[own, :end], ((1,), (0,)))
        m_ref[own, :end] = block
        if end < n:
            panel = exact(a_ref[rest, own], inverse, ((1,), (1,)))
            a_ref[rest, rest] = a_ref[rest, rest] - exact(panel, panel, ((1,), (1,)))
            m_ref[rest, :end] = m_ref[rest, :end] - exact(panel, block, ((1,), (0,)))

    for copy in z_rep:
        copy.wait_recv()
    new = exact(z_all[...].reshape(N_REP * 16, n), m_ref[...], ((1,), (1,)))
    lane = lax.broadcasted_iota(jnp.int32, (16, 128), 1) // 32
    for zz in range(N_ROW):
        base = 128 * (zz // 4)
        tile_out = jnp.zeros((16, 128), F32)
        for q in range(N_REP):
            block = new[16 * q : 16 * q + 16, base : base + 128]
            turn = (32 * (q - zz % 4)) % 128
            if turn:
                block = pltpu.roll(block, turn, 1)
            tile_out = jnp.where(lane == q, block, tile_out)
        packed[zz] = tile_out.astype(BF16)
    fac_ref[row] = packed[row]
    last = [
        start(packed.at[peer["row"]], fac_ref.at[row], fs.at[o], fr.at[o], peer) for o, peer in enumerate(row_peers)
    ]
    basis_ref[...] = exact(sk[...].astype(F32), m_ref[...], ((1,), (1,)))
    for copy in last:
        copy.wait_recv()
    for copy in sends:
        copy.wait_send()


def find_range(part, second):
    dma = pltpu.SemaphoreType.DMA
    vmem = pl.BlockSpec(memory_space=pltpu.VMEM)
    rows, rank = part.shape
    counts = (7, 7, 3, 15, 7, 15, 16)
    sems = []
    for count in counts:
        sems += [dma((count,))] * 2
    sems += [dma((2,)), dma((2,)), dma, dma, dma((15,)), dma((15,)), dma((3,)), dma((3,)), dma((15,)), dma((15,))]
    return pl.pallas_call(
        range_kernel,
        out_shape=(
            jax.ShapeDtypeStruct((rows, rank), F32),
            jax.ShapeDtypeStruct((N_ROW, 16, 128), BF16),
        ),
        in_specs=[vmem] * 2,
        out_specs=(vmem,) * 2,
        scratch_shapes=[
            pltpu.VMEM((rows, rank), BF16),
            pltpu.VMEM((N_COL - 1, rows // N_COL, rank), BF16),
            pltpu.VMEM((rows, rank), BF16),
            pltpu.VMEM((rank, rank), F32),
            pltpu.VMEM((rank, rank), F32),
            pltpu.VMEM((3, 16, rank), F32),
            pltpu.VMEM((8, 8, 128), F32),
            pltpu.VMEM((N_ROW, 8, 128), F32),
            pltpu.VMEM((N_ROW, N_REP, 16, rank), F32),
            pltpu.VMEM((2, N_ROW, 16, rank), F32),
            pltpu.VMEM((N_ROW, 16, rank), BF16),
            pltpu.VMEM((N_ROW - 1, 16, rank), F32),
            pltpu.VMEM((N_REP, 16, rank), F32),
            pltpu.VMEM((N_ROW, 16, 128), BF16),
            pltpu.VMEM((rank, rank), F32),
            pltpu.VMEM((rank, rank), F32),
            pltpu.VMEM((N_ROW, 16, rank), BF16),
            pltpu.VMEM((N_ROW, 16, rank), F32),
        ]
        + sems,
        compiler_params=pltpu.CompilerParams(collective_id=1, has_side_effects=True, vmem_limit_bytes=40 << 20),
        name="find_range",
    )(part, second)


def shards(tokens, out_grad, moment_old, basis_old, factor_old, test_matrix):
    moment, second, part = tile(tokens[0], out_grad[0], factor_old.T, moment_old, basis_old, test_matrix)
    basis_new, blocks = find_range(part, second)
    rank = factor_old.shape[1]
    factor_new = blocks.reshape(N_ROW, 16, N_REP, rank).transpose(0, 2, 1, 3).reshape(-1, rank).astype(F32)
    return (moment, basis_new, factor_new)


def solution(mesh):
    placed = (
        P("rep", "col", "row"),
        P("rep", "row", "col"),
        P(("row", "rep"), "col"),
        P(("row", "rep"), None),
        P("col", "row"),
        P("col", None),
    )
    return jax.shard_map(
        shards,
        mesh=mesh,
        in_specs=placed,
        out_specs=(P(("row", "rep"), "col"), P(("row", "rep"), None), P("col", "row")),
        check_vma=False,
    )
```

```python
import functools

import jax
import jax.numpy as jnp
from jax import lax
from jax.experimental import pallas as pl
from jax.experimental.pallas import tpu as pltpu
from jax.sharding import PartitionSpec as P

MESH = pl.DeviceIdType.MESH
F32 = jnp.float32
BF16 = jnp.bfloat16
N_ROW, N_COL, N_REP = 16, 8, 4


def remote(src, dst, send, recv, device):
    return pltpu.make_async_remote_copy(
        src_ref=src, dst_ref=dst, send_sem=send, recv_sem=recv, device_id=device, device_id_type=MESH
    )


def greet(devices):
    barrier = pltpu.get_barrier_semaphore()
    for device in devices:
        pl.semaphore_signal(barrier, inc=1, device_id=device, device_id_type=MESH)
    pl.semaphore_wait(barrier, len(devices))


def others(axis, size):
    me = lax.axis_index(axis)
    return [{axis: lax.rem(me + o, size)} for o in range(1, size)]


HOPS = (
    (0, 4), (0, 8), (0, 12), (0, 1), (0, -1), (0, 2),
    (4, 1), (4, -1), (4, 2), (4, -2),
    (8, 1), (8, -1), (8, -2),
    (12, 1), (12, -1),
)
NEAR = ((0, 1, 2), (3, 6, 10, 13), (4, 7, 11, 14), (5, 8, 9, 12))


def tile_kernel(
    tok_ref, og_ref, fa_ref, moment_ref, basis_ref, test_ref, new_ref, second_ref, part_ref,
    tk, g, f, old_f, old_m, old_b, test, high, low, zs, zr, xs, xr, ss, sr, ts, tr, cs, cr, local,
):
    row, col, rep = lax.axis_index("row"), lax.axis_index("col"), lax.axis_index("rep")
    half, core = rep // 2, lax.rem(rep, 2)
    across = (1 - half) * 2 + core
    sibling = half * 2 + 1 - core
    corner = (1 - half) * 2 + 1 - core
    rep_peers = others("rep", N_REP)
    col_peers = others("col", N_COL)

    def at(offset):
        return lax.rem(row + N_ROW + offset, N_ROW)

    wide = tok_ref.shape[1] // N_REP
    part = pl.ds(pl.multiple_of(rep * wide, wide), wide)
    own = [
        pltpu.make_async_copy(og_ref, g.at[rep, row // 4, lax.rem(row, 4)], local.at[0]),
        pltpu.make_async_copy(fa_ref, old_f, local.at[1]),
        pltpu.make_async_copy(tok_ref.at[:, part], tk.at[col, rep], local.at[2]),
        pltpu.make_async_copy(moment_ref, old_m, local.at[3]),
        pltpu.make_async_copy(basis_ref, old_b, local.at[4]),
        pltpu.make_async_copy(test_ref, test, local.at[5]),
    ]
    for copy in own:
        copy.start()
    plane = []
    for h in range(2):
        for o in range(N_COL):
            if h or o:
                plane.append({"col": lax.rem(col + o, N_COL), "rep": lax.rem(half + h, 2) * 2 + core})
    greet(rep_peers + others("row", N_ROW) + plane)

    def slot(stream, z):
        if stream:
            return f.at[z // 4, lax.rem(z, 4), core]
        return g.at[rep, z // 4, lax.rem(z, 4)]

    def hop(stream, i, arriving=False):
        d, o = HOPS[i]
        here = slot(stream, at(d - o if arriving else d))
        return remote(here, here, zs.at[stream, i], zr.at[stream, i], {"row": at(o)})

    classes = [lax.rem(row + 4 + o, 4) for o in (0, -1, 1, 2)]

    def over(j, arriving=False):
        here = g.at[across if arriving else rep, :, classes[j]]
        return remote(here, here, xs.at[j], xr.at[j], {"rep": across})

    def hand(kind, j, arriving=False):
        if kind == 2:
            here = f.at[:, classes[j], (1 - core) if arriving else core]
        elif kind == 1:
            here = g.at[corner if arriving else across, :, classes[j]]
        else:
            here = g.at[sibling if arriving else rep, :, classes[j]]
        return remote(here, here, ss.at[kind, j], sr.at[kind, j], {"rep": sibling})

    sends = []

    def go(copy):
        copy.start()
        sends.append(copy)

    own[0].wait()
    for i in range(6):
        go(hop(0, i))
    first = []
    for o, peer in enumerate(rep_peers):
        there = pl.ds(pl.multiple_of(peer["rep"] * wide, wide), wide)
        copy = remote(tok_ref.at[:, there], tk.at[col, rep], ts.at[o], tr.at[o], peer)
        go(copy)
        first.append(copy)
    own[1].wait()
    f[row // 4, lax.rem(row, 4), core] = old_f[pl.ds(pl.multiple_of(16 * core, 16), 16)].astype(BF16)
    for i in range(6):
        go(hop(1, i))
    for stream in range(2):
        for i, onward in ((0, (13, 14)), (2, (6, 7, 8, 9)), (1, (10, 11, 12))):
            hop(stream, i, True).wait_recv()
            for k in onward:
                go(hop(stream, k))
        if stream == 0:
            go(over(0))
            go(hand(0, 0))
            own[2].wait()
            for copy in first:
                copy.wait_recv()
            second = []
            for o, peer in enumerate(col_peers):
                copy = remote(tk.at[col], tk.at[col], cs.at[o], cr.at[o], peer)
                go(copy)
                second.append(copy)
        else:
            go(hand(2, 0))
    for j in (1, 2, 3):
        for i in NEAR[j]:
            hop(0, i, True).wait_recv()
        go(over(j))
        go(hand(0, j))
    for j in (0, 1):
        over(j, True).wait_recv()
        go(hand(1, j))
    for j in (1, 2, 3):
        for i in NEAR[j]:
            hop(1, i, True).wait_recv()
        go(hand(2, j))
    for j in (2, 3):
        over(j, True).wait_recv()
        go(hand(1, j))
    for copy in own[3:]:
        copy.wait()
    high[...] = old_b[...].astype(BF16)
    low[...] = (old_b[...] - high[...].astype(F32)).astype(BF16)
    part_ref[...] = jnp.zeros_like(part_ref)
    for copy in second:
        copy.wait_recv()
    for j in range(4):
        for kind in range(3):
            hand(kind, j, True).wait_recv()

    step = 256
    rank = old_b.shape[1]

    def columns(i, carry):
        here = pl.ds(pl.multiple_of(i * step, step), step)
        gradient = jnp.zeros((new_ref.shape[0], step), F32)
        for b in range(N_REP):
            left = tk[:, b].reshape(-1, wide)
            right = g[b, :, :, :, here].reshape(-1, step)
            piece = lax.dot_general(left, right, (((0,), (0,)), ((), ())), preferred_element_type=F32)
            gradient = gradient + piece.astype(BF16).astype(F32)
        new_ref[:, here] = 0.9 * old_m[:, here] + 0.1 * gradient
        factor = f[:, :, :, :, here].reshape(rank, step)
        previous = jnp.dot(high[...], factor, preferred_element_type=F32)
        previous = previous + jnp.dot(low[...], factor, preferred_element_type=F32)
        second_tile = (0.95 * previous + 0.05 * gradient * gradient).astype(BF16)
        second_ref[:, here] = second_tile
        part_ref[...] += jnp.dot(second_tile, test[here], preferred_element_type=F32)
        return carry

    lax.fori_loop(0, new_ref.shape[1] // step, columns, 0)
    for copy in sends:
        copy.wait_send()


SPAN = 128


def invert_diagonal(block):
    sub = lax.broadcasted_iota(jnp.int32, (8, SPAN), 0)
    shape = (SPAN, SPAN)
    d = block
    x = (lax.broadcasted_iota(jnp.int32, shape, 0) == lax.broadcasted_iota(jnp.int32, shape, 1)).astype(F32)
    out = []

    def spread(value):
        return jnp.broadcast_to(value, (8, SPAN))

    for j0 in range(0, SPAN, 8):
        wide = [spread(d[:8, j0 + m : j0 + m + 1]) for m in range(8)]
        s = [[spread(wide[m][i : i + 1, :]) if m <= i else None for m in range(8)] for i in range(8)]
        p = [spread(d[i : i + 1, :]) for i in range(8)]
        q = [spread(x[i : i + 1, :]) for i in range(8)]
        inverse = [None] * 8
        f = [[None] * 8 for _ in range(8)]
        for m in range(8):
            guess = pl.reciprocal(s[m][m], approx=True)
            inverse[m] = guess * (2.0 - s[m][m] * guess)
            for i in range(m + 1, 8):
                f[i][m] = s[i][m] * inverse[m]
            for i in range(m + 1, 8):
                for l in range(m + 1, i + 1):
                    s[i][l] = s[i][l] - f[i][m] * s[l][m]
            for i in range(m + 1, 8):
                p[i] = p[i] - f[i][m] * p[m]
                q[i] = q[i] - f[i][m] * q[m]
        done = q[0] * lax.rsqrt(s[0][0])
        for i in range(1, 8):
            done = jnp.where(sub == i, q[i] * lax.rsqrt(s[i][i]), done)
        out.append(done)
        if j0 + 8 == SPAN:
            break
        v, w = [None] * 8, [None] * 8
        for i in reversed(range(8)):
            v[i] = p[i] * inverse[i]
            w[i] = q[i] * inverse[i]
            for m in range(i + 1, 8):
                v[i] = v[i] - f[m][i] * v[m]
                w[i] = w[i] - f[m][i] * w[m]
        d, x = d[8:], x[8:]
        source = d
        for m in range(8):
            c = source[:, j0 + m : j0 + m + 1]
            d = d - c * v[m][:1]
            x = x - c * w[m][:1]
    return jnp.concatenate(out, 0)


def exact(a, b, dims):
    return lax.dot_general(a, b, (dims, ((), ())), precision=lax.Precision.HIGHEST, preferred_element_type=F32)


def range_kernel(
    part_ref, second_ref, basis_ref, fac_ref,
    send_sk, land_sk, sk, gram, out, land1, tiles, land2, z, land_c, land_x, land_z, z_all, packed, m_ref, a_ref, away_x, z_half,
    s1, r1, s2, r2, s3, r3, s4, r4, s5, r5, s6, r6, s7, r7, zs1, zr1, zs2, zr2, zs3, zr3, zs4, zr4, fs, fr,
):
    row, col, rep = lax.axis_index("row"), lax.axis_index("col"), lax.axis_index("rep")
    half, core = rep // 2, lax.rem(rep, 2)
    rep_peers = others("rep", N_REP)
    row_peers = others("row", N_ROW)
    col_peers = others("col", N_COL)
    sibling = {"rep": half * 2 + 1 - core}
    across = {"rep": (1 - half) * 2 + core}
    plane = []
    for h in range(2):
        for o in range(N_COL):
            if h or o:
                plane.append({"col": lax.rem(col + o, N_COL), "rep": lax.rem(half + h, 2) * 2 + core})
    sends = []

    def start(src, dst, send, recv, device):
        copy = remote(src, dst, send, recv, device)
        copy.start()
        sends.append(copy)
        return copy

    send_sk[...] = part_ref[...].astype(BF16)
    rows = part_ref.shape[0] // N_COL
    mine = pl.ds(pl.multiple_of(col * rows, rows), rows)
    copies = []
    for o, peer in enumerate(col_peers):
        there = pl.ds(pl.multiple_of(peer["col"] * rows, rows), rows)
        copies.append(start(send_sk.at[there], land_sk.at[o], s1.at[o], r1.at[o], peer))
    total = part_ref[mine]
    for o in range(N_COL - 1):
        copies[o].wait_recv()
        total = total + land_sk[o].astype(F32)
    sk[mine] = total.astype(BF16)
    copies = [start(sk.at[mine], sk.at[mine], s2.at[o], r2.at[o], peer) for o, peer in enumerate(col_peers)]
    for copy in copies:
        copy.wait_recv()

    sketch = sk[...]
    gram[...] = lax.dot_general(sketch, sketch, (((0,), (0,)), ((), ())), preferred_element_type=F32)
    copies = []
    for o, peer in enumerate(rep_peers):
        there = pl.ds(pl.multiple_of(col * 64 + peer["rep"] * 16, 16), 16)
        copies.append(start(gram.at[there], land1.at[o], s3.at[o], r3.at[o], peer))

    for i in range(4):
        piece = lax.dot_general(
            second_ref[:, 256 * i : 256 * i + 256], sketch, (((0,), (0,)), ((), ())), preferred_element_type=F32
        )
        z[4 * i : 4 * i + 4] = piece.reshape(4, N_REP, 16, sketch.shape[1])

    strip = pl.multiple_of(col * 64 + rep * 16, 16)
    total = gram[pl.ds(strip, 16)]
    for o in range(N_REP - 1):
        copies[o].wait_recv()
        total = total + land1[o]
    for t in range(8):
        tiles[t] = total[8 * (t // 4) : 8 * (t // 4) + 8, 128 * (t % 4) : 128 * (t % 4) + 128]
    tile_no = lax.rem(row, 8)
    copies = []
    for o, peer in enumerate(row_peers):
        copies.append(start(tiles.at[lax.rem(peer["row"], 8)], land2.at[row], s4.at[o], r4.at[o], peer))
    land2[row] = tiles[tile_no]

    z_core = [
        start(z.at[:, 2 * h + 1 - core], land_c.at[h], zs1.at[h], zr1.at[h], sibling) for h in range(2)
    ]

    for copy in z_core:
        copy.wait_recv()

    def add_core(i, carry):
        away_x[i] = (land_c[1 - half, i] + z[i, 2 * (1 - half) + core]).astype(BF16)
        return carry

    lax.fori_loop(0, N_ROW, add_core, 0)
    z_across = start(away_x, land_x, zs2, zr2, across)

    for o in range(N_ROW - 1):
        copies[o].wait_recv()
    total = land2[0]
    for i in range(1, N_ROW):
        total = total + land2[i]
    spot = (
        pl.ds(pl.multiple_of(strip + 8 * (tile_no // 4), 8), 8),
        pl.ds(pl.multiple_of(128 * lax.rem(tile_no, 4), 128), 128),
    )
    out[spot] = total
    copies = []
    for i, o in enumerate((1, 2, 3, -1, -2, -3, -4)):
        peer = {"row": lax.rem(row + N_ROW + o, N_ROW)}
        copies.append(start(out.at[spot], out.at[spot], s5.at[i], r5.at[i], peer))

    for copy in copies:
        copy.wait_recv()
    here = out.at[pl.ds(strip, 16)]
    copies = [start(here, here, s6.at[i], r6.at[i], peer) for i, peer in enumerate(plane)]
    onward = [start(here, here, s7.at[15], r7.at[15], sibling)]
    z_row = []

    def add_across(i, carry):
        z_half[i] = (land_x[i].astype(F32) + land_c[half, i]) + z[i, 2 * half + core]
        return carry

    for h in range(2):
        if h == 1:
            z_across.wait_recv()
            lax.fori_loop(0, N_ROW, add_across, 0)
            for o, peer in enumerate(row_peers):
                z_row.append(start(z_half.at[peer["row"]], land_z.at[o], zs3.at[o], zr3.at[o], peer))
        for o in range(N_COL):
            if h or o:
                i = h * N_COL + o - 1
                first = lax.rem(col + N_COL - o, N_COL) * 64 + (lax.rem(half + h, 2) * 2 + core) * 16
                there = out.at[pl.ds(pl.multiple_of(first, 16), 16)]
                copies[i].wait_recv()
                onward.append(start(there, there, s7.at[i], r7.at[i], sibling))

    for copy in onward:
        copy.wait_recv()

    n = gram.shape[0]
    eye = lax.broadcasted_iota(jnp.int32, (n, n), 0) == lax.broadcasted_iota(jnp.int32, (n, n), 1)
    whole = out[...]
    shift = 0.01 * jnp.sum(jnp.where(eye, whole, 0.0)) / n
    a_ref[...] = jnp.where(eye, whole + shift, whole)
    m_ref[...] = jnp.where(eye, 1.0, 0.0).astype(F32)
    z_rep = []
    for k in range(n // SPAN):
        end = (k + 1) * SPAN
        own, rest = slice(k * SPAN, end), slice(end, n)
        if end == n:
            z_sum = z_half[row]
            for o in range(N_ROW - 1):
                z_row[o].wait_recv()
                z_sum = z_sum + land_z[o]
            z_all[rep] = z_sum
            for o, peer in enumerate(rep_peers):
                z_rep.append(start(z_all.at[rep], z_all.at[rep], zs4.at[o], zr4.at[o], peer))
        inverse = invert_diagonal(a_ref[own, own])
        block = exact(inverse, m_ref[own, :end], ((1,), (0,)))
        m_ref[own, :end] = block
        if end < n:
            panel = exact(a_ref[rest, own], inverse, ((1,), (1,)))
            a_ref[rest, rest] = a_ref[rest, rest] - exact(panel, panel, ((1,), (1,)))
            m_ref[rest, :end] = m_ref[rest, :end] - exact(panel, block, ((1,), (0,)))

    for copy in z_rep:
        copy.wait_recv()
    new = exact(z_all[...].reshape(N_REP * 16, n), m_ref[...], ((1,), (1,)))
    lane = lax.broadcasted_iota(jnp.int32, (16, 128), 1) // 32
    for zz in range(N_ROW):
        base = 128 * (zz // 4)
        tile_out = jnp.zeros((16, 128), F32)
        for q in range(N_REP):
            block = new[16 * q : 16 * q + 16, base : base + 128]
            turn = (32 * (q - zz % 4)) % 128
            if turn:
                block = pltpu.roll(block, turn, 1)
            tile_out = jnp.where(lane == q, block, tile_out)
        packed[zz] = tile_out.astype(BF16)
    fac_ref[row] = packed[row]
    last = [
        start(packed.at[peer["row"]], fac_ref.at[row], fs.at[o], fr.at[o], peer) for o, peer in enumerate(row_peers)
    ]
    basis_ref[...] = exact(sk[...].astype(F32), m_ref[...], ((1,), (1,)))
    for copy in last:
        copy.wait_recv()
    for copy in sends:
        copy.wait_send()


def whole_kernel(*refs):
    inputs, new_ref, basis_ref, fac_ref = refs[:6], refs[6], refs[7], refs[8]
    second, part = refs[9:11]
    tile_kernel(*inputs, new_ref, second, part, *refs[11:31])
    range_kernel(part, second, basis_ref, fac_ref, *refs[31:])


def whole(tokens, out_grad, factor, moment_old, basis_old, test_matrix):
    dma = pltpu.SemaphoreType.DMA
    vmem = pl.BlockSpec(memory_space=pltpu.VMEM)
    hbm = pl.BlockSpec(memory_space=pltpu.HBM)
    depth, wide = tokens.shape[0], tokens.shape[1] // N_REP
    tall = out_grad.shape[0]
    rows, columns = moment_old.shape
    rank = basis_old.shape[1]
    sems = []
    for count in (7, 7, 3, 15, 7, 15, 16):
        sems += [dma((count,))] * 2
    sems += [dma((2,)), dma((2,)), dma, dma, dma((15,)), dma((15,)), dma((3,)), dma((3,)), dma((15,)), dma((15,))]
    return pl.pallas_call(
        whole_kernel,
        out_shape=(
            jax.ShapeDtypeStruct((rows, columns), F32),
            jax.ShapeDtypeStruct((rows, rank), F32),
            jax.ShapeDtypeStruct((N_ROW, 16, 128), BF16),
        ),
        in_specs=[hbm] * 6,
        out_specs=(vmem,) * 3,
        scratch_shapes=[
            pltpu.VMEM((rows, columns), BF16),
            pltpu.VMEM((rows, rank), F32),
            pltpu.VMEM((N_COL, N_REP, depth, wide), BF16),
            pltpu.VMEM((N_REP, 4, 4, tall, columns), BF16),
            pltpu.VMEM((4, 4, 2, factor.shape[0] // 2, columns), BF16),
            pltpu.VMEM(factor.shape, F32),
            pltpu.VMEM(moment_old.shape, F32),
            pltpu.VMEM(basis_old.shape, F32),
            pltpu.VMEM(test_matrix.shape, BF16),
            pltpu.VMEM((rows, rank), BF16),
            pltpu.VMEM((rows, rank), BF16),
            dma((2, 15)), dma((2, 15)), dma((4,)), dma((4,)), dma((3, 4)), dma((3, 4)),
            dma((3,)), dma((3,)), dma((7,)), dma((7,)), dma((6,)),
            pltpu.VMEM((rows, rank), BF16),
            pltpu.VMEM((N_COL - 1, rows // N_COL, rank), BF16),
            pltpu.VMEM((rows, rank), BF16),
            pltpu.VMEM((rank, rank), F32),
            pltpu.VMEM((rank, rank), F32),
            pltpu.VMEM((3, 16, rank), F32),
            pltpu.VMEM((8, 8, 128), F32),
            pltpu.VMEM((N_ROW, 8, 128), F32),
            pltpu.VMEM((N_ROW, N_REP, 16, rank), F32),
            pltpu.VMEM((2, N_ROW, 16, rank), F32),
            pltpu.VMEM((N_ROW, 16, rank), BF16),
            pltpu.VMEM((N_ROW - 1, 16, rank), F32),
            pltpu.VMEM((N_REP, 16, rank), F32),
            pltpu.VMEM((N_ROW, 16, 128), BF16),
            pltpu.VMEM((rank, rank), F32),
            pltpu.VMEM((rank, rank), F32),
            pltpu.VMEM((N_ROW, 16, rank), BF16),
            pltpu.VMEM((N_ROW, 16, rank), F32),
        ]
        + sems,
        compiler_params=pltpu.CompilerParams(collective_id=1, has_side_effects=True, vmem_limit_bytes=54 << 20),
        name="whole",
    )(tokens, out_grad, factor, moment_old, basis_old, test_matrix)


def shards(tokens, out_grad, moment_old, basis_old, factor_old, test_matrix):
    moment, basis_new, blocks = whole(tokens[0], out_grad[0], factor_old.T, moment_old, basis_old, test_matrix)
    rank = factor_old.shape[1]
    factor_new = blocks.reshape(N_ROW, 16, N_REP, rank).transpose(0, 2, 1, 3).reshape(-1, rank).astype(F32)
    return (moment, basis_new, factor_new)


def solution(mesh):
    placed = (
        P("rep", "col", "row"),
        P("rep", "row", "col"),
        P(("row", "rep"), "col"),
        P(("row", "rep"), None),
        P("col", "row"),
        P("col", None),
    )
    return jax.shard_map(
        shards,
        mesh=mesh,
        in_specs=placed,
        out_specs=(P(("row", "rep"), "col"), P(("row", "rep"), None), P("col", "row")),
        check_vma=False,
    )
```

```python
import functools

import jax
import jax.numpy as jnp
from jax import lax
from jax.experimental import pallas as pl
from jax.experimental.pallas import tpu as pltpu
from jax.sharding import PartitionSpec as P

MESH = pl.DeviceIdType.MESH
F32 = jnp.float32
BF16 = jnp.bfloat16
N_ROW, N_COL, N_REP = 16, 8, 4


def remote(src, dst, send, recv, device):
    return pltpu.make_async_remote_copy(
        src_ref=src, dst_ref=dst, send_sem=send, recv_sem=recv, device_id=device, device_id_type=MESH
    )


def greet(devices):
    barrier = pltpu.get_barrier_semaphore()
    for device in devices:
        pl.semaphore_signal(barrier, inc=1, device_id=device, device_id_type=MESH)
    pl.semaphore_wait(barrier, len(devices))


def others(axis, size):
    me = lax.axis_index(axis)
    return [{axis: lax.rem(me + o, size)} for o in range(1, size)]


HOPS = (
    (0, 4), (0, 8), (0, 12), (0, 1), (0, -1), (0, 2),
    (4, 1), (4, -1), (4, 2), (4, -2),
    (8, 1), (8, -1), (8, -2),
    (12, 1), (12, -1),
)
NEAR = ((0, 1, 2), (3, 6, 10, 13), (4, 7, 11, 14), (5, 8, 9, 12))


def tile_kernel(
    tok_ref, og_ref, fa_ref, moment_ref, basis_ref, test_ref, new_ref, second_ref, part_ref,
    tk, g, f, old_f, old_m, old_b, test, high, low, zs, zr, xs, xr, ss, sr, ts, tr, cs, cr, local,
):
    row, col, rep = lax.axis_index("row"), lax.axis_index("col"), lax.axis_index("rep")
    half, core = rep // 2, lax.rem(rep, 2)
    across = (1 - half) * 2 + core
    sibling = half * 2 + 1 - core
    corner = (1 - half) * 2 + 1 - core
    rep_peers = others("rep", N_REP)
    col_peers = others("col", N_COL)

    def at(offset):
        return lax.rem(row + N_ROW + offset, N_ROW)

    wide = tok_ref.shape[1] // N_REP
    part = pl.ds(pl.multiple_of(rep * wide, wide), wide)
    own = [
        pltpu.make_async_copy(og_ref, g.at[rep, row // 4, lax.rem(row, 4)], local.at[0]),
        pltpu.make_async_copy(fa_ref, old_f, local.at[1]),
        pltpu.make_async_copy(tok_ref.at[:, part], tk.at[col, rep], local.at[2]),
        pltpu.make_async_copy(moment_ref, old_m, local.at[3]),
        pltpu.make_async_copy(basis_ref, old_b, local.at[4]),
        pltpu.make_async_copy(test_ref, test, local.at[5]),
    ]
    for copy in own:
        copy.start()
    plane = []
    for h in range(2):
        for o in range(N_COL):
            if h or o:
                plane.append({"col": lax.rem(col + o, N_COL), "rep": lax.rem(half + h, 2) * 2 + core})
    greet(rep_peers + others("row", N_ROW) + plane)

    def slot(stream, z):
        if stream:
            return f.at[z // 4, lax.rem(z, 4), core]
        return g.at[rep, z // 4, lax.rem(z, 4)]

    def hop(stream, i, arriving=False):
        d, o = HOPS[i]
        here = slot(stream, at(d - o if arriving else d))
        return remote(here, here, zs.at[stream, i], zr.at[stream, i], {"row": at(o)})

    classes = [lax.rem(row + 4 + o, 4) for o in (0, -1, 1, 2)]

    def over(j, arriving=False):
        here = g.at[across if arriving else rep, :, classes[j]]
        return remote(here, here, xs.at[j], xr.at[j], {"rep": across})

    def hand(kind, j, arriving=False):
        if kind == 2:
            here = f.at[:, classes[j], (1 - core) if arriving else core]
        elif kind == 1:
            here = g.at[corner if arriving else across, :, classes[j]]
        else:
            here = g.at[sibling if arriving else rep, :, classes[j]]
        return remote(here, here, ss.at[kind, j], sr.at[kind, j], {"rep": sibling})

    sends = []

    def go(copy):
        copy.start()
        sends.append(copy)

    own[0].wait()
    for i in range(6):
        go(hop(0, i))
    first = []
    for o, peer in enumerate(rep_peers):
        there = pl.ds(pl.multiple_of(peer["rep"] * wide, wide), wide)
        copy = remote(tok_ref.at[:, there], tk.at[col, rep], ts.at[o], tr.at[o], peer)
        go(copy)
        first.append(copy)
    own[1].wait()
    f[row // 4, lax.rem(row, 4), core] = old_f[pl.ds(pl.multiple_of(16 * core, 16), 16)].astype(BF16)
    def pass_on(stream):
        for i, onward in ((0, (13, 14)), (2, (6, 7, 8, 9)), (1, (10, 11, 12))):
            hop(stream, i, True).wait_recv()
            for k in onward:
                go(hop(stream, k))

    pass_on(0)
    for i in range(6):
        go(hop(1, i))
    go(over(0))
    go(hand(0, 0))
    own[2].wait()
    for copy in first:
        copy.wait_recv()
    second = []
    for o, peer in enumerate(col_peers):
        copy = remote(tk.at[col], tk.at[col], cs.at[o], cr.at[o], peer)
        go(copy)
        second.append(copy)
    for j in (1, 2, 3):
        for i in NEAR[j]:
            hop(0, i, True).wait_recv()
        go(over(j))
        go(hand(0, j))
    pass_on(1)
    go(hand(2, 0))
    for j in (0, 1):
        over(j, True).wait_recv()
        go(hand(1, j))
    for j in (1, 2, 3):
        for i in NEAR[j]:
            hop(1, i, True).wait_recv()
        go(hand(2, j))
    for j in (2, 3):
        over(j, True).wait_recv()
        go(hand(1, j))
    for copy in own[3:]:
        copy.wait()
    high[...] = old_b[...].astype(BF16)
    low[...] = (old_b[...] - high[...].astype(F32)).astype(BF16)
    part_ref[...] = jnp.zeros_like(part_ref)
    for copy in second:
        copy.wait_recv()
    for j in range(4):
        for kind in range(3):
            hand(kind, j, True).wait_recv()

    step = 256
    rank = old_b.shape[1]

    def columns(i, carry):
        here = pl.ds(pl.multiple_of(i * step, step), step)
        gradient = jnp.zeros((new_ref.shape[0], step), F32)
        for b in range(N_REP):
            left = tk[:, b].reshape(-1, wide)
            right = g[b, :, :, :, here].reshape(-1, step)
            piece = lax.dot_general(left, right, (((0,), (0,)), ((), ())), preferred_element_type=F32)
            gradient = gradient + piece.astype(BF16).astype(F32)
        new_ref[:, here] = 0.9 * old_m[:, here] + 0.1 * gradient
        factor = f[:, :, :, :, here].reshape(rank, step)
        previous = jnp.dot(high[...], factor, preferred_element_type=F32)
        previous = previous + jnp.dot(low[...], factor, preferred_element_type=F32)
        second_tile = (0.95 * previous + 0.05 * gradient * gradient).astype(BF16)
        second_ref[:, here] = second_tile
        part_ref[...] += jnp.dot(second_tile, test[here], preferred_element_type=F32)
        return carry

    lax.fori_loop(0, new_ref.shape[1] // step, columns, 0)
    for copy in sends:
        copy.wait_send()


SPAN = 128


def invert_diagonal(block):
    sub = lax.broadcasted_iota(jnp.int32, (8, SPAN), 0)
    shape = (SPAN, SPAN)
    d = block
    x = (lax.broadcasted_iota(jnp.int32, shape, 0) == lax.broadcasted_iota(jnp.int32, shape, 1)).astype(F32)
    out = []

    def spread(value):
        return jnp.broadcast_to(value, (8, SPAN))

    for j0 in range(0, SPAN, 8):
        wide = [spread(d[:8, j0 + m : j0 + m + 1]) for m in range(8)]
        s = [[spread(wide[m][i : i + 1, :]) if m <= i else None for m in range(8)] for i in range(8)]
        p = [spread(d[i : i + 1, :]) for i in range(8)]
        q = [spread(x[i : i + 1, :]) for i in range(8)]
        inverse = [None] * 8
        f = [[None] * 8 for _ in range(8)]
        for m in range(8):
            guess = pl.reciprocal(s[m][m], approx=True)
            inverse[m] = guess * (2.0 - s[m][m] * guess)
            for i in range(m + 1, 8):
                f[i][m] = s[i][m] * inverse[m]
            for i in range(m + 1, 8):
                for l in range(m + 1, i + 1):
                    s[i][l] = s[i][l] - f[i][m] * s[l][m]
            for i in range(m + 1, 8):
                p[i] = p[i] - f[i][m] * p[m]
                q[i] = q[i] - f[i][m] * q[m]
        done = q[0] * lax.rsqrt(s[0][0])
        for i in range(1, 8):
            done = jnp.where(sub == i, q[i] * lax.rsqrt(s[i][i]), done)
        out.append(done)
        if j0 + 8 == SPAN:
            break
        v, w = [None] * 8, [None] * 8
        for i in reversed(range(8)):
            v[i] = p[i] * inverse[i]
            w[i] = q[i] * inverse[i]
            for m in range(i + 1, 8):
                v[i] = v[i] - f[m][i] * v[m]
                w[i] = w[i] - f[m][i] * w[m]
        d, x = d[8:], x[8:]
        source = d
        for m in range(8):
            c = source[:, j0 + m : j0 + m + 1]
            d = d - c * v[m][:1]
            x = x - c * w[m][:1]
    return jnp.concatenate(out, 0)


def exact(a, b, dims):
    return lax.dot_general(a, b, (dims, ((), ())), precision=lax.Precision.HIGHEST, preferred_element_type=F32)


def range_kernel(
    part_ref, second_ref, basis_ref, fac_ref,
    send_sk, land_sk, sk, gram, out, land1, tiles, land2, z, land_c, land_x, land_z, z_all, packed, m_ref, a_ref, away_x, z_half,
    s1, r1, s2, r2, s3, r3, s4, r4, s5, r5, s6, r6, s7, r7, zs1, zr1, zs2, zr2, zs3, zr3, zs4, zr4, fs, fr,
):
    row, col, rep = lax.axis_index("row"), lax.axis_index("col"), lax.axis_index("rep")
    half, core = rep // 2, lax.rem(rep, 2)
    rep_peers = others("rep", N_REP)
    row_peers = others("row", N_ROW)
    col_peers = others("col", N_COL)
    sibling = {"rep": half * 2 + 1 - core}
    across = {"rep": (1 - half) * 2 + core}
    plane = []
    for h in range(2):
        for o in range(N_COL):
            if h or o:
                plane.append({"col": lax.rem(col + o, N_COL), "rep": lax.rem(half + h, 2) * 2 + core})
    sends = []

    def start(src, dst, send, recv, device):
        copy = remote(src, dst, send, recv, device)
        copy.start()
        sends.append(copy)
        return copy

    send_sk[...] = part_ref[...].astype(BF16)
    rows = part_ref.shape[0] // N_COL
    mine = pl.ds(pl.multiple_of(col * rows, rows), rows)
    copies = []
    for o, peer in enumerate(col_peers):
        there = pl.ds(pl.multiple_of(peer["col"] * rows, rows), rows)
        copies.append(start(send_sk.at[there], land_sk.at[o], s1.at[o], r1.at[o], peer))
    total = part_ref[mine]
    for o in range(N_COL - 1):
        copies[o].wait_recv()
        total = total + land_sk[o].astype(F32)
    sk[mine] = total.astype(BF16)
    copies = [start(sk.at[mine], sk.at[mine], s2.at[o], r2.at[o], peer) for o, peer in enumerate(col_peers)]
    for copy in copies:
        copy.wait_recv()

    sketch = sk[...]
    gram[...] = lax.dot_general(sketch, sketch, (((0,), (0,)), ((), ())), preferred_element_type=F32)
    copies = []
    for o, peer in enumerate(rep_peers):
        there = pl.ds(pl.multiple_of(col * 64 + peer["rep"] * 16, 16), 16)
        copies.append(start(gram.at[there], land1.at[o], s3.at[o], r3.at[o], peer))

    for i in range(4):
        piece = lax.dot_general(
            second_ref[:, 256 * i : 256 * i + 256], sketch, (((0,), (0,)), ((), ())), preferred_element_type=F32
        )
        z[4 * i : 4 * i + 4] = piece.reshape(4, N_REP, 16, sketch.shape[1])

    strip = pl.multiple_of(col * 64 + rep * 16, 16)
    total = gram[pl.ds(strip, 16)]
    for o in range(N_REP - 1):
        copies[o].wait_recv()
        total = total + land1[o]
    for t in range(8):
        tiles[t] = total[8 * (t // 4) : 8 * (t // 4) + 8, 128 * (t % 4) : 128 * (t % 4) + 128]
    tile_no = lax.rem(row, 8)
    copies = []
    for o, peer in enumerate(row_peers):
        copies.append(start(tiles.at[lax.rem(peer["row"], 8)], land2.at[row], s4.at[o], r4.at[o], peer))
    land2[row] = tiles[tile_no]

    z_core = [
        start(z.at[:, 2 * h + 1 - core], land_c.at[h], zs1.at[h], zr1.at[h], sibling) for h in range(2)
    ]

    for copy in z_core:
        copy.wait_recv()

    def add_core(i, carry):
        away_x[i] = (land_c[1 - half, i] + z[i, 2 * (1 - half) + core]).astype(BF16)
        return carry

    lax.fori_loop(0, N_ROW, add_core, 0)
    z_across = start(away_x, land_x, zs2, zr2, across)

    for o in range(N_ROW - 1):
        copies[o].wait_recv()
    total = land2[0]
    for i in range(1, N_ROW):
        total = total + land2[i]
    spot = (
        pl.ds(pl.multiple_of(strip + 8 * (tile_no // 4), 8), 8),
        pl.ds(pl.multiple_of(128 * lax.rem(tile_no, 4), 128), 128),
    )
    out[spot] = total
    copies = []
    for i, o in enumerate((1, 2, 3, -1, -2, -3, -4)):
        peer = {"row": lax.rem(row + N_ROW + o, N_ROW)}
        copies.append(start(out.at[spot], out.at[spot], s5.at[i], r5.at[i], peer))

    for copy in copies:
        copy.wait_recv()
    here = out.at[pl.ds(strip, 16)]
    copies = [start(here, here, s6.at[i], r6.at[i], peer) for i, peer in enumerate(plane)]
    onward = [start(here, here, s7.at[15], r7.at[15], sibling)]
    z_row = []

    def add_across(i, carry):
        z_half[i] = (land_x[i].astype(F32) + land_c[half, i]) + z[i, 2 * half + core]
        return carry

    for h in range(2):
        if h == 1:
            z_across.wait_recv()
            lax.fori_loop(0, N_ROW, add_across, 0)
            for o, peer in enumerate(row_peers):
                z_row.append(start(z_half.at[peer["row"]], land_z.at[o], zs3.at[o], zr3.at[o], peer))
        for o in range(N_COL):
            if h or o:
                i = h * N_COL + o - 1
                first = lax.rem(col + N_COL - o, N_COL) * 64 + (lax.rem(half + h, 2) * 2 + core) * 16
                there = out.at[pl.ds(pl.multiple_of(first, 16), 16)]
                copies[i].wait_recv()
                onward.append(start(there, there, s7.at[i], r7.at[i], sibling))

    for copy in onward:
        copy.wait_recv()

    n = gram.shape[0]
    eye = lax.broadcasted_iota(jnp.int32, (n, n), 0) == lax.broadcasted_iota(jnp.int32, (n, n), 1)
    whole = out[...]
    shift = 0.01 * jnp.sum(jnp.where(eye, whole, 0.0)) / n
    a_ref[...] = jnp.where(eye, whole + shift, whole)
    m_ref[...] = jnp.where(eye, 1.0, 0.0).astype(F32)
    z_rep = []
    for k in range(n // SPAN):
        end = (k + 1) * SPAN
        own, rest = slice(k * SPAN, end), slice(end, n)
        if end == n:
            z_sum = z_half[row]
            for o in range(N_ROW - 1):
                z_row[o].wait_recv()
                z_sum = z_sum + land_z[o]
            z_all[rep] = z_sum
            for o, peer in enumerate(rep_peers):
                z_rep.append(start(z_all.at[rep], z_all.at[rep], zs4.at[o], zr4.at[o], peer))
        inverse = invert_diagonal(a_ref[own, own])
        block = exact(inverse, m_ref[own, :end], ((1,), (0,)))
        m_ref[own, :end] = block
        if end < n:
            panel = exact(a_ref[rest, own], inverse, ((1,), (1,)))
            a_ref[rest, rest] = a_ref[rest, rest] - exact(panel, panel, ((1,), (1,)))
            m_ref[rest, :end] = m_ref[rest, :end] - exact(panel, block, ((1,), (0,)))

    for copy in z_rep:
        copy.wait_recv()
    new = exact(z_all[...].reshape(N_REP * 16, n), m_ref[...], ((1,), (1,)))
    lane = lax.broadcasted_iota(jnp.int32, (16, 128), 1) // 32
    for zz in range(N_ROW):
        base = 128 * (zz // 4)
        tile_out = jnp.zeros((16, 128), F32)
        for q in range(N_REP):
            block = new[16 * q : 16 * q + 16, base : base + 128]
            turn = (32 * (q - zz % 4)) % 128
            if turn:
                block = pltpu.roll(block, turn, 1)
            tile_out = jnp.where(lane == q, block, tile_out)
        packed[zz] = tile_out.astype(BF16)
    fac_ref[row] = packed[row]
    last = [
        start(packed.at[peer["row"]], fac_ref.at[row], fs.at[o], fr.at[o], peer) for o, peer in enumerate(row_peers)
    ]
    basis_ref[...] = exact(sk[...].astype(F32), m_ref[...], ((1,), (1,)))
    for copy in last:
        copy.wait_recv()
    for copy in sends:
        copy.wait_send()


def whole_kernel(*refs):
    inputs, new_ref, basis_ref, fac_ref = refs[:6], refs[6], refs[7], refs[8]
    second, part = refs[9:11]
    tile_kernel(*inputs, new_ref, second, part, *refs[11:31])
    range_kernel(part, second, basis_ref, fac_ref, *refs[31:])


def whole(tokens, out_grad, factor, moment_old, basis_old, test_matrix):
    dma = pltpu.SemaphoreType.DMA
    vmem = pl.BlockSpec(memory_space=pltpu.VMEM)
    hbm = pl.BlockSpec(memory_space=pltpu.HBM)
    depth, wide = tokens.shape[0], tokens.shape[1] // N_REP
    tall = out_grad.shape[0]
    rows, columns = moment_old.shape
    rank = basis_old.shape[1]
    sems = []
    for count in (7, 7, 3, 15, 7, 15, 16):
        sems += [dma((count,))] * 2
    sems += [dma((2,)), dma((2,)), dma, dma, dma((15,)), dma((15,)), dma((3,)), dma((3,)), dma((15,)), dma((15,))]
    return pl.pallas_call(
        whole_kernel,
        out_shape=(
            jax.ShapeDtypeStruct((rows, columns), F32),
            jax.ShapeDtypeStruct((rows, rank), F32),
            jax.ShapeDtypeStruct((N_ROW, 16, 128), BF16),
        ),
        in_specs=[hbm] * 6,
        out_specs=(vmem,) * 3,
        scratch_shapes=[
            pltpu.VMEM((rows, columns), BF16),
            pltpu.VMEM((rows, rank), F32),
            pltpu.VMEM((N_COL, N_REP, depth, wide), BF16),
            pltpu.VMEM((N_REP, 4, 4, tall, columns), BF16),
            pltpu.VMEM((4, 4, 2, factor.shape[0] // 2, columns), BF16),
            pltpu.VMEM(factor.shape, F32),
            pltpu.VMEM(moment_old.shape, F32),
            pltpu.VMEM(basis_old.shape, F32),
            pltpu.VMEM(test_matrix.shape, BF16),
            pltpu.VMEM((rows, rank), BF16),
            pltpu.VMEM((rows, rank), BF16),
            dma((2, 15)), dma((2, 15)), dma((4,)), dma((4,)), dma((3, 4)), dma((3, 4)),
            dma((3,)), dma((3,)), dma((7,)), dma((7,)), dma((6,)),
            pltpu.VMEM((rows, rank), BF16),
            pltpu.VMEM((N_COL - 1, rows // N_COL, rank), BF16),
            pltpu.VMEM((rows, rank), BF16),
            pltpu.VMEM((rank, rank), F32),
            pltpu.VMEM((rank, rank), F32),
            pltpu.VMEM((3, 16, rank), F32),
            pltpu.VMEM((8, 8, 128), F32),
            pltpu.VMEM((N_ROW, 8, 128), F32),
            pltpu.VMEM((N_ROW, N_REP, 16, rank), F32),
            pltpu.VMEM((2, N_ROW, 16, rank), F32),
            pltpu.VMEM((N_ROW, 16, rank), BF16),
            pltpu.VMEM((N_ROW - 1, 16, rank), F32),
            pltpu.VMEM((N_REP, 16, rank), F32),
            pltpu.VMEM((N_ROW, 16, 128), BF16),
            pltpu.VMEM((rank, rank), F32),
            pltpu.VMEM((rank, rank), F32),
            pltpu.VMEM((N_ROW, 16, rank), BF16),
            pltpu.VMEM((N_ROW, 16, rank), F32),
        ]
        + sems,
        compiler_params=pltpu.CompilerParams(collective_id=1, has_side_effects=True, vmem_limit_bytes=54 << 20),
        name="whole",
    )(tokens, out_grad, factor, moment_old, basis_old, test_matrix)


def shards(tokens, out_grad, moment_old, basis_old, factor_old, test_matrix):
    moment, basis_new, blocks = whole(tokens[0], out_grad[0], factor_old.T, moment_old, basis_old, test_matrix)
    rank = factor_old.shape[1]
    factor_new = blocks.reshape(N_ROW, 16, N_REP, rank).transpose(0, 2, 1, 3).reshape(-1, rank).astype(F32)
    return (moment, basis_new, factor_new)


def solution(mesh):
    placed = (
        P("rep", "col", "row"),
        P("rep", "row", "col"),
        P(("row", "rep"), "col"),
        P(("row", "rep"), None),
        P("col", "row"),
        P("col", None),
    )
    return jax.shard_map(
        shards,
        mesh=mesh,
        in_specs=placed,
        out_specs=(P(("row", "rep"), "col"), P(("row", "rep"), None), P("col", "row")),
        check_vma=False,
    )
```
